32 devices in a mesh: dp: 8 (over z, x), mp: 4 (over y, core).
Axes of the slice: x: 2, y: 2, z: 4, core: 2. Of those that a mesh axis runs over, the one named last changes fastest.
Arguments:
- tokens: bfloat16 [32768, 1024], P(('dp', 'mp')), may hold values from -6 to 6
- lengths: int32 [32], P(('dp', 'mp')), may hold values from 10 to 1024, as said below
- key_mask: int32 [32768], P(('dp', 'mp')), may hold values 0 or 1
- w_query: bfloat16 [1024, 1024], replicated, may hold values from -0.1875 to 0.1875
- w_key: bfloat16 [1024, 1024], replicated, may hold values from -0.1875 to 0.1875
- w_value: bfloat16 [1024, 1024], replicated, may hold values from -0.1875 to 0.1875
- w_output: bfloat16 [1024, 1024], replicated, may hold values from -1.5 to 1.5
- norm1_gain: bfloat16 [1024], replicated, may hold values from 0.5 to 1.5
- norm1_shift: bfloat16 [1024], replicated, may hold values from -1.5 to 1.5
- w_in: bfloat16 [1024, 4096], P(None, 'mp'), may hold values from -0.1875 to 0.1875
- b_in: bfloat16 [4096], P('mp'), may hold values from -2.5 to 2.5
- w_out: bfloat16 [4096, 1024], P('mp'), may hold values from -0.09375 to 0.09375
- norm2_gain: bfloat16 [1024], replicated, may hold values from 0.5 to 1.5
- norm2_shift: bfloat16 [1024], replicated, may hold values from -1.5 to 1.5
- prefix_key: bfloat16 [64, 1024], replicated, may hold values from -6 to 6
- prefix_value: bfloat16 [64, 1024], replicated, may hold values from -6 to 6
- out_grad: bfloat16 [32768, 1024], P(('dp', 'mp')), may hold values from -6 to 6
Outputs:
- output: bfloat16 [32768, 1024], P(('dp', 'mp'))
- input_grad: bfloat16 [32768, 1024], P(('dp', 'mp'))
- prefix_key_grad: float32 [64, 1024], P(None, 'mp')
- prefix_value_grad: float32 [64, 1024], P(None, 'mp')
The draws below stay inside these ranges and needn't reach their ends.
Inputs may be any that keep to these rules, and one draw needn't show every extreme that they name: `lengths`: some slot holds a sentence of exactly 1024 tokens and another one of exactly 10.
All inputs are finite; a program needn't handle non-finite values. No bound on the sum of `key_mask` on one device may be relied on, other than what follows from the above.
Results may differ from the reference program's by a relative error of at most 0.014.
Values may be sent and summed in bfloat16 or wider, within the bound.
A program may use at most 256 MiB of HBM per device.

```python
import math
import jax
import jax.numpy as jnp
from jax import lax

D = 1024
HEADS = 16
HEAD = 64
FF = 4096
PREFIX = 64
SLOT = 1024
LEAST = 10
SLOTS = 32
TOKENS = 32768


def draw_lengths(key, part):
    key = jax.random.fold_in(key, 7)
    first_key, second_key, place_key, other_key = jax.random.split(key, 4)
    first = jax.random.randint(first_key, (SLOTS,), LEAST, SLOT + 1)
    second = jax.random.randint(second_key, (SLOTS,), LEAST, SLOT + 1)
    longest = jax.random.randint(place_key, (), 0, SLOTS)
    shortest = (longest + 1 + jax.random.randint(other_key, (), 0, SLOTS - 1)) % SLOTS
    places = jnp.arange(SLOTS, dtype=jnp.int32)
    drawn = jnp.maximum(first, second)
    drawn = jnp.where(places == longest, SLOT, drawn)
    drawn = jnp.where(places == shortest, LEAST, drawn)
    return drawn.astype(jnp.int32)


def place_ends(values, key, least, top_value):
    spot = [jax.random.randint(jax.random.fold_in(key, axis), (), 0, length) for axis, length in enumerate(values.shape)]
    main_axis = values.shape.index(max(values.shape))
    beside = spot[:main_axis] + [(spot[main_axis] + 1) % values.shape[main_axis]] + spot[main_axis + 1:]
    return values.at[tuple(spot)].set(least).at[tuple(beside)].set(top_value)


def level_of(key, dims, shards, low, top_value):
    def one(dim, shards_of):
        heights = jax.random.uniform(jax.random.fold_in(jax.random.fold_in(key, 6), dim), (shards_of,), jnp.float32, low / len(shards), top_value / len(shards))
        return jnp.repeat(jnp.exp(heights), dims[dim] // shards_of).reshape((-1,) + (1,) * (len(dims) - dim - 1))

    factor_of = one(*shards[0])
    for cut in shards[1:]:
        factor_of = factor_of * one(*cut)
    return factor_of


def gaussian(key, shape, scale, limit, cuts=(), held_as=jnp.bfloat16):
    values = jax.random.normal(key, shape, jnp.float32) * scale
    if len(cuts) > 0:
        values = level_of(key, shape, cuts, -0.22, 0.18) * values
    return jnp.clip(values, min=-limit, max=limit).astype(held_as)


def setup_inputs(seed: int = 0) -> dict:
    key_list = jax.random.split(jax.random.key(seed), 18)
    tokens = gaussian(key_list[0], (TOKENS, D), 1.0, 6.0, ((0, 32),))
    lengths = draw_lengths(jax.random.fold_in(key_list[17], 71), 0)
    key_mask = place_ends((jax.random.randint(key_list[2], (TOKENS,), 0, 8) < 7).astype(jnp.int32), jax.random.fold_in(key_list[2], 1), 0, 1)
    w_query = gaussian(key_list[3], (D, D), D ** -0.5, 0.1875)
    w_key = gaussian(key_list[4], (D, D), D ** -0.5, 0.1875)
    w_value = gaussian(key_list[5], (D, D), D ** -0.5, 0.1875)
    w_output = gaussian(key_list[6], (D, D), (D // 64) ** -0.5, 1.5)
    norm1_gain = jnp.clip(1.0 + 0.1 * jax.random.normal(key_list[7], (D,), jnp.float32), 0.5, 1.5).astype(jnp.bfloat16)
    norm1_shift = gaussian(key_list[8], (D,), 0.3, 1.5)
    w_in = gaussian(key_list[9], (D, FF), D ** -0.5, 0.1875, ((1, 4),))
    b_in = gaussian(key_list[10], (FF,), 0.5, 2.5, ((0, 4),))
    w_out = gaussian(key_list[11], (FF, D), FF ** -0.5, 0.09375, ((0, 4),))
    norm2_gain = jnp.clip(1.0 + 0.1 * jax.random.normal(key_list[12], (D,), jnp.float32), 0.5, 1.5).astype(jnp.bfloat16)
    norm2_shift = gaussian(key_list[13], (D,), 0.3, 1.5)
    prefix_key = gaussian(key_list[14], (PREFIX, D), 1.0, 6.0)
    prefix_value = gaussian(key_list[15], (PREFIX, D), 1.0, 6.0)
    out_grad = gaussian(key_list[16], (TOKENS, D), 1.0, 6.0, ((0, 32),))
    return {"tokens": tokens, "lengths": lengths, "key_mask": key_mask, "w_query": w_query, "w_key": w_key, "w_value": w_value, "w_output": w_output, "norm1_gain": norm1_gain, "norm1_shift": norm1_shift, "w_in": w_in, "b_in": b_in, "w_out": w_out, "norm2_gain": norm2_gain, "norm2_shift": norm2_shift, "prefix_key": prefix_key, "prefix_value": prefix_value, "out_grad": out_grad}


@jax.custom_vjp
def low(v):
    return lax.optimization_barrier(v.astype(jnp.bfloat16)).astype(jnp.float32)

@jax.custom_vjp
def low_back(v):
    return v

def low_keep(v):
    return (low(v), None)

def low_pass(kept, grad):
    return (grad,)

def back_keep(v):
    return (v, None)

def back_low(kept, grad):
    return (low(grad),)
low.defvjp(low_keep, low_pass)
low_back.defvjp(back_keep, back_low)
highest = lax.Precision.HIGHEST
epsilon = 1e-05
masked_score = -1e+30

def layer_norm(hidden_rows, gain, shift):
    middle = lax.optimization_barrier(jnp.mean(hidden_rows, axis=-1, keepdims=True))
    centered = hidden_rows - middle
    spread = lax.optimization_barrier(jnp.mean(centered * centered, axis=-1, keepdims=True))
    return centered * lax.rsqrt(spread + epsilon) * gain + shift

def matmul(left, right):
    return jnp.dot(left, right, precision=highest)

def attend_slot(prefix_key, prefix_value, item):
    queries, keys_own, values_own, live_own = item
    keys = jnp.concatenate([prefix_key, keys_own], axis=0).reshape(PREFIX + SLOT, HEADS, HEAD)
    values = jnp.concatenate([prefix_value, values_own], axis=0).reshape(PREFIX + SLOT, HEADS, HEAD)
    live = jnp.concatenate([jnp.ones((PREFIX,), dtype=bool), live_own])
    scale = 1.0 / math.sqrt(HEAD)
    raw = jnp.einsum('qhd,khd->hqk', queries.reshape(SLOT, HEADS, HEAD), keys, precision=highest)
    scores = low_back(raw * scale)
    scores = jnp.where(live[None, None, :], scores, masked_score)
    probs = low(jax.nn.softmax(scores, axis=-1))
    context = jnp.einsum('hqk,khd->qhd', probs, values, precision=highest)
    return context.reshape(SLOT, HEADS * HEAD)

def block_forward(rows_in, prefix_key, prefix_value, live_rows, params):
    w_query, w_key, w_value, w_output, gain_one, shift_one, w_in, b_in, w_out, gain_two, shift_two = params
    count = live_rows.shape[0]
    queries = low_back(low(matmul(rows_in, w_query)))
    keys_own = low_back(low(matmul(rows_in, w_key)))
    values_own = low_back(low(matmul(rows_in, w_value)))

    def slot_function(item):
        return attend_slot(prefix_key, prefix_value, item)
    context = lax.map(jax.checkpoint(slot_function), (queries.reshape(count, SLOT, HEADS * HEAD), keys_own.reshape(count, SLOT, HEADS * HEAD), values_own.reshape(count, SLOT, HEADS * HEAD), live_rows))
    context = low_back(low(context.reshape(count * SLOT, HEADS * HEAD)))
    mixed = rows_in + low_back(matmul(context, w_output))
    normed = layer_norm(mixed, gain_one, shift_one)
    pre = low_back(matmul(low(normed), w_in) + b_in)
    active = low(jax.nn.gelu(pre, approximate=False))
    summed = normed + low_back(matmul(active, w_out))
    return layer_norm(summed, gain_two, shift_two)

def reference(tokens, lengths, key_mask, w_query, w_key, w_value, w_output, norm1_gain, norm1_shift, w_in, b_in, w_out, norm2_gain, norm2_shift, prefix_key, prefix_value, out_grad):
    params = tuple((array.astype(jnp.float32) for array in (w_query, w_key, w_value, w_output, norm1_gain, norm1_shift, w_in, b_in, w_out, norm2_gain, norm2_shift)))
    prefix_keys = prefix_key.astype(jnp.float32)
    prefix_values = prefix_value.astype(jnp.float32)
    positions = jnp.arange(SLOT, dtype=jnp.int32)
    live = (positions[None, :] < lengths[:, None]) & (key_mask.reshape(SLOTS, SLOT) > 0)
    group = math.gcd(SLOTS, max(1, 4096 // SLOT))
    blocks = SLOTS // group
    rows_all = tokens.astype(jnp.float32).reshape(blocks, group * SLOT, HEADS * HEAD)
    grads_all = out_grad.astype(jnp.float32).reshape(blocks, group * SLOT, HEADS * HEAD)
    live_all = live.reshape(blocks, group, SLOT)

    def advance(carry, item):
        block_rows, block_grads, block_live = item

        def forward(rows_in, key_part, value_part):
            return block_forward(rows_in, key_part, value_part, block_live, params)
        result, pull = jax.vjp(forward, block_rows, prefix_keys, prefix_values)
        row_grad, key_grad, value_grad = pull(block_grads)
        return ((carry[0] + key_grad, carry[1] + value_grad), (result.astype(jnp.bfloat16), row_grad.astype(jnp.bfloat16)))
    zeros = jnp.zeros((PREFIX, HEADS * HEAD), jnp.float32)
    (key_total, value_total), (outputs, input_grads) = lax.scan(advance, (zeros, zeros), (rows_all, grads_all, live_all))
    return (outputs.reshape(TOKENS, HEADS * HEAD), input_grads.reshape(TOKENS, HEADS * HEAD), key_total, value_total)
```

```python
import functools
import math

import jax
import jax.numpy as jnp
from jax import lax
from jax.experimental import pallas as pl
from jax.experimental.pallas import tpu as pltpu
from jax.sharding import PartitionSpec as P

HEADS = 16
HEAD = 64
PREFIX = 64
SLOT = 1024
GROUP = 4
TILE = 256

EPSILON = 1e-05
MASKED = -1e30
LOG2E = 1.4426950408889634
BF = jnp.bfloat16
F32 = jnp.float32

VMEM = pl.BlockSpec(memory_space=pltpu.VMEM)
SMEM = pl.BlockSpec(memory_space=pltpu.SMEM)
HBM = pl.BlockSpec(memory_space=pl.ANY)


def dg(left, right, left_dim, right_dim):
    return lax.dot_general(
        left, right, (((left_dim,), (right_dim,)), ((), ())), preferred_element_type=F32
    )


def rows_at(start, size):
    return pl.ds(pl.multiple_of(start, size), size)


def block_diagonal(part):
    stacked = jnp.concatenate([part] * GROUP, axis=0)
    head_of_row = lax.broadcasted_iota(jnp.int32, stacked.shape, 0) // HEAD
    head_of_column = lax.broadcasted_iota(jnp.int32, stacked.shape, 1) // HEAD
    return jnp.where(head_of_row == head_of_column, stacked, jnp.zeros_like(stacked))


def diagonal_rows(blocks):
    head_of_row = lax.broadcasted_iota(jnp.int32, blocks.shape, 0) // HEAD
    head_of_column = lax.broadcasted_iota(jnp.int32, blocks.shape, 1) // HEAD
    kept = jnp.where(head_of_row == head_of_column, blocks, jnp.zeros_like(blocks))
    return kept[:64] + kept[64:128] + kept[128:192] + kept[192:]


def ones_rows(width):
    row = lax.broadcasted_iota(jnp.int32, (16, width), 0)
    return jnp.where(row == 0, 1.0, 0.0).astype(BF)


def project(tokens, w_query, w_key, w_value, query_t, key, key_t, value, value_t):
    width = tokens.shape[1]

    @pl.loop(0, width // TILE)
    def _(j):
        cols = rows_at(j * TILE, TILE)
        part = jnp.dot(tokens[...], w_query[:, cols], preferred_element_type=F32)
        query_t[cols, :] = (part * (LOG2E / math.sqrt(HEAD))).astype(BF).T
        part = jnp.dot(tokens[...], w_key[:, cols], preferred_element_type=F32).astype(BF)
        key[:, cols] = part
        key_t[cols, :] = part.T
        part = jnp.dot(tokens[...], w_value[:, cols], preferred_element_type=F32).astype(BF)
        value[:, cols] = part
        value_t[cols, :] = part.T


def mask_block(length, mask_ref, mask_cols):
    place = lax.broadcasted_iota(jnp.int32, (1, SLOT), 1)
    live = (place < length) & (mask_ref[...] > 0)
    bias = jnp.where(live, 0.0, MASKED)
    row = lax.broadcasted_iota(jnp.int32, (128, SLOT), 0)
    mask_cols[...] = jnp.where(row == 0, bias, 0.0).T.astype(BF)


def attend(query_t, key, value_t, mask_cols, prefix_key, prefix_value, weights_hbm, weights_prefix,
           context_t, inverse, scores_a, scores_b, scores_prefix, peak_prefix, peaks, sums, totals,
           weights_a, weights_b, sems):
    tiles = SLOT // TILE
    pairs = HEADS // 2

    @pl.loop(0, HEADS // GROUP)
    def _(g):
        cols = rows_at(g * 256, 256)
        s = jnp.dot(block_diagonal(prefix_key[:, cols]), query_t[cols, :], preferred_element_type=F32)
        scores_prefix[cols, :] = s
        peak_prefix[g] = jnp.concatenate(
            [jnp.max(s[i * 64 : i * 64 + 64], axis=0, keepdims=True) for i in range(GROUP)]
            + [jnp.zeros((4, SLOT), F32)], axis=0)

    def right_side(h, half):
        q = query_t[rows_at(h * HEAD, HEAD), :]
        zero = jnp.zeros_like(q)
        last = jnp.concatenate([ones_rows(SLOT), jnp.zeros((112, SLOT), BF)], axis=0)
        return jnp.concatenate([q, zero, last] if half == 0 else [zero, q, last], axis=0)

    def score_tile(h, t, right):
        rows = slice(t * TILE, (t + 1) * TILE)
        left = jnp.concatenate([key[rows, rows_at((h // 2) * 128, 128)], mask_cols[rows, :]], axis=1)
        return jnp.dot(left, right, preferred_element_type=F32)

    def folded(s):
        return jnp.max(s.reshape(TILE // 8, 8, SLOT), axis=0)

    def set_peak(h, half, peak):
        group = peak_prefix[h // GROUP]
        row = lax.broadcasted_iota(jnp.int32, group.shape, 0)
        own = jnp.max(jnp.where(row == h % GROUP, group, -jnp.inf), axis=0, keepdims=True)
        peaks[half : half + 1, :] = jnp.maximum(jnp.max(peak, axis=0, keepdims=True), own)

    def head_step(h, half, scores_new, scores_old, staged, more):
        if more:
            right = right_side(h + 1, 1 - half)
        top = peaks[half : half + 1, :]
        rows_h = rows_at(h * HEAD, HEAD)
        left = jnp.concatenate([value_t[rows_h, :], ones_rows(SLOT)], axis=0)
        total = jnp.zeros((80, SLOT), F32)
        peak = None
        for t in range(tiles):
            rows = slice(t * TILE, (t + 1) * TILE)
            if more:
                s = score_tile(h + 1, t, right)
                scores_new[rows, :] = s
                f = folded(s)
                peak = f if peak is None else jnp.maximum(peak, f)
            p = jnp.exp2(scores_old[rows, :] - top).astype(BF)
            staged[rows, :] = p
            total += jnp.dot(left[:, rows], p, preferred_element_type=F32)
        weights_prefix[rows_h, :] = jnp.exp2(scores_prefix[rows_h, :] - top).astype(BF)
        if more:
            set_peak(h + 1, 1 - half, peak)
        sums[rows_h, :] = total[:HEAD]
        totals[pl.ds(h, 1), :] = total[HEAD : HEAD + 1]

    right = right_side(0, 0)
    peak = None
    for t in range(tiles):
        s = score_tile(0, t, right)
        scores_a[t * TILE : (t + 1) * TILE, :] = s
        f = folded(s)
        peak = f if peak is None else jnp.maximum(peak, f)
    set_peak(0, 0, peak)

    def copy_out(h, half):
        return pltpu.make_async_copy((weights_a, weights_b)[half], weights_hbm.at[h], sems.at[half])

    @pl.loop(0, pairs - 1)
    def _(i):
        h = i * 2
        for half in range(2):
            @pl.when(i > 0)
            def _():
                copy_out(h + half - 2, half).wait()
            if half == 0:
                head_step(h, 0, scores_b, scores_a, weights_a, True)
            else:
                head_step(h + 1, 1, scores_a, scores_b, weights_b, True)
            copy_out(h + half, half).start()

    h = HEADS - 2
    copy_out(h - 2, 0).wait()
    head_step(h, 0, scores_b, scores_a, weights_a, True)
    copy_out(h, 0).start()
    copy_out(h - 1, 1).wait()
    head_step(h + 1, 1, scores_a, scores_b, weights_b, False)
    copy_out(h + 1, 1).start()

    @pl.loop(0, HEADS // GROUP)
    def _(g):
        cols = rows_at(g * 256, 256)
        head_of_row = lax.broadcasted_iota(jnp.int32, (256, 128), 0) // HEAD
        head_of_column = lax.broadcasted_iota(jnp.int32, (256, 128), 1)
        counts = jnp.where(head_of_row == head_of_column, 1.0, 0.0).astype(BF)
        left = jnp.concatenate([block_diagonal(prefix_value[:, cols]), counts], axis=1)
        both = dg(left, weights_prefix[cols, :], 0, 0)
        for i in range(GROUP):
            h = g * GROUP + i
            scale = 1.0 / (totals[pl.ds(h, 1), :] + both[256 + i : 257 + i, :])
            inverse[pl.ds(h, 1), :] = scale
            rows_h = rows_at(h * HEAD, HEAD)
            context_t[rows_h, :] = (
                (sums[rows_h, :] + both[i * HEAD : (i + 1) * HEAD]) * scale
            ).astype(BF)

    copy_out(HEADS - 2, 0).wait()
    copy_out(HEADS - 1, 1).wait()


def forward_kernel(length, mask_ref, tokens, w_query, w_key, w_value, prefix_key, prefix_value,
                   weights_hbm, weights_prefix, query_t, key_t, value, context_t, inverse,
                   key, value_t, mask_cols, scores_a, scores_b, scores_prefix, peak_prefix, peaks,
                   sums, totals, weights_a, weights_b, sems):
    mask_block(length[0], mask_ref, mask_cols)
    project(tokens, w_query, w_key, w_value, query_t, key, key_t, value, value_t)
    attend(query_t, key, value_t, mask_cols, prefix_key, prefix_value, weights_hbm, weights_prefix,
           context_t, inverse, scores_a, scores_b, scores_prefix, peak_prefix, peaks, sums, totals,
           weights_a, weights_b, sems)


def norm_parts(rows):
    centered = rows - jnp.mean(rows, axis=-1, keepdims=True)
    spread = jnp.mean(centered * centered, axis=-1, keepdims=True)
    inverse = lax.rsqrt(spread + EPSILON)
    return centered * inverse, inverse


def norm_back(scaled, unit, inverse):
    first = jnp.mean(scaled, axis=-1, keepdims=True)
    second = jnp.mean(scaled * unit, axis=-1, keepdims=True)
    return inverse * (scaled - first - unit * second)


def gelu_parts(v):
    u = v * (1.0 / math.sqrt(2.0))
    normal = 0.5 * lax.erf(u) + 0.5
    bell = jnp.exp2((u * u) * (-LOG2E))
    return (v * normal).astype(BF), (normal + (u * bell) * (1.0 / math.sqrt(math.pi))).astype(BF)


def middle_kernel(tokens, context_t, inverse, w_output, vectors, w_in, b_in, w_out, out_grad,
                  output, lower, grad_t, centre,
                  unit, inverse_one, low, total, active, slope):
    shards, width, hidden = w_in.shape
    rows = tokens.shape[0]
    gain_one, shift_one = vectors[0:1, :], vectors[1:2, :]
    gain_two, shift_two = vectors[2:3, :], vectors[3:4, :]

    @pl.loop(0, rows // TILE)
    def _(r):
        rs = rows_at(r * TILE, TILE)
        mixed = tokens[rs, :].astype(F32) + dg(context_t[:, rs], w_output[...], 0, 0)
        u, inv = norm_parts(mixed)
        unit[rs, :] = u
        inverse_one[rs, :] = inv
        normed = u * gain_one + shift_one
        total[rs, :] = normed
        low[rs, :] = normed.astype(BF)

    def first_parts(j):
        def part(c):
            cols = slice(c * TILE, (c + 1) * TILE)
            pre = jnp.dot(low[...], w_in[j, :, cols], preferred_element_type=F32) + b_in[j, 0:1, cols]
            act, slo = gelu_parts(pre)
            active[j % 2, :, cols] = act
            slope[j, :, cols] = slo
        return [functools.partial(part, c) for c in range(hidden // TILE)]

    def second_parts(j):
        def part(c):
            cols = slice(c * TILE, (c + 1) * TILE)
            total[:, cols] += jnp.dot(active[j % 2], w_out[j, :, cols], preferred_element_type=F32)
        return [functools.partial(part, c) for c in range(width // TILE)]

    def run(*lists):
        for k in range(max(len(parts) for parts in lists)):
            for parts in lists:
                if k < len(parts):
                    parts[k]()

    run(first_parts(0))

    @pl.loop(1, shards)
    def _(j):
        run(first_parts(j), second_parts(j - 1))

    run(second_parts(shards - 1))

    @pl.loop(0, rows // TILE)
    def _(r):
        rs = rows_at(r * TILE, TILE)
        u, inv = norm_parts(total[rs, :])
        output[rs, :] = (u * gain_two + shift_two).astype(BF)
        upper = norm_back(out_grad[rs, :].astype(F32) * gain_two, u, inv)
        total[rs, :] = upper
        low[rs, :] = upper.astype(BF)

    def third_parts(j):
        def part(c):
            cols = slice(c * TILE, (c + 1) * TILE)
            grad = dg(low[...], w_out[j, cols, :], 1, 1)
            active[j % 2, :, cols] = (grad * slope[j, :, cols].astype(F32)).astype(BF)
        return [functools.partial(part, c) for c in range(hidden // TILE)]

    def fourth_parts(j):
        def part(c):
            cols = slice(c * TILE, (c + 1) * TILE)
            total[:, cols] += dg(active[j % 2], w_in[j, cols, :], 1, 1)
        return [functools.partial(part, c) for c in range(width // TILE)]

    run(third_parts(0))

    @pl.loop(1, shards)
    def _(j):
        run(third_parts(j), fourth_parts(j - 1))

    run(fourth_parts(shards - 1))

    @pl.loop(0, rows // TILE)
    def _(r):
        rs = rows_at(r * TILE, TILE)
        grad = norm_back(total[rs, :] * gain_one, unit[rs, :], inverse_one[rs, :])
        lower[rs, :] = grad
        low[rs, :] = grad.astype(BF)

    @pl.loop(0, width // TILE)
    def _(g):
        gs = rows_at(g * TILE, TILE)
        grad = dg(w_output[gs, :], low[...], 1, 1)
        for i in range(TILE // HEAD):
            h = g * (TILE // HEAD) + i
            rows_h = rows_at(h * HEAD, HEAD)
            scaled = grad[i * HEAD : (i + 1) * HEAD] * inverse[pl.ds(h, 1), :]
            grad_t[rows_h, :] = scaled.astype(BF)
            middle = -jnp.sum(scaled * context_t[rows_h, :].astype(F32), axis=0, keepdims=True)
            high = middle.astype(BF)
            rest = (middle - high.astype(F32)).astype(BF)
            row = lax.broadcasted_iota(jnp.int32, (16, SLOT), 0)
            both = jnp.where(row == 0, high.astype(F32), jnp.where(row == 1, rest.astype(F32), 0.0))
            centre[rows_at(h * 16, 16), :] = both.astype(BF)


def backward_kernel(weights_hbm, weights_prefix, query_t, key_t, value, grad_t, centre, prefix_key,
                    prefix_value, lower, w_query, w_key, w_value,
                    input_grad, prefix_grads,
                    query_back, key_back, value_back, query_prefix, staged, sems):
    tiles = SLOT // TILE
    ln2 = 1.0 / LOG2E

    def copy_in(h, half):
        return pltpu.make_async_copy(weights_hbm.at[h], staged.at[half], sems.at[half])

    copy_in(0, 0).start()

    @pl.loop(0, HEADS // GROUP)
    def _(g):
        cols = rows_at(g * 256, 256)
        keys = block_diagonal(prefix_key[:, cols])
        values = block_diagonal(prefix_value[:, cols])
        grads = grad_t[cols, :]
        back = jnp.dot(values, grads, preferred_element_type=F32)
        parts = []
        for i in range(GROUP):
            middle = jnp.sum(centre[rows_at((g * GROUP + i) * 16, 16), :].astype(F32), axis=0, keepdims=True)
            rows_h = rows_at((g * GROUP + i) * HEAD, HEAD)
            parts.append(
                (weights_prefix[rows_h, :].astype(F32) * (back[i * HEAD : (i + 1) * HEAD] + middle)).astype(BF)
            )
        back = jnp.concatenate(parts, axis=0)
        prefix_grads[:PREFIX, cols] = diagonal_rows(dg(back, query_t[cols, :], 1, 1)) * ln2
        prefix_grads[PREFIX:, cols] = diagonal_rows(dg(weights_prefix[cols, :], grads, 1, 1))
        query_prefix[cols, :] = dg(keys, back, 0, 0)

    lane = lax.broadcasted_iota(jnp.int32, (TILE, 128), 1)
    pick = jnp.where(lane < 2, 1.0, 0.0).astype(BF)

    def head_step(h, half):
        rows_h = rows_at(h * HEAD, HEAD)
        pair = rows_at((h // 2) * 128, 128)
        grads = grad_t[rows_h, :]
        zero = jnp.zeros_like(grads)
        last = jnp.concatenate([centre[rows_at(h * 16, 16), :], jnp.zeros((112, SLOT), BF)], axis=0)
        right = jnp.concatenate([grads, zero, last] if half == 0 else [zero, grads, last], axis=0)
        queries = query_t[rows_h, :]
        keys = key_t[rows_h, :]
        total = query_prefix[rows_h, :]
        for t in range(tiles):
            rows = slice(t * TILE, (t + 1) * TILE)
            left = jnp.concatenate([value[rows, pair], pick], axis=1)
            back = jnp.dot(left, right, preferred_element_type=F32)
            w = staged[half, rows, :]
            back = (back * w.astype(F32)).astype(BF)
            value_back[rows_h, rows] = dg(grads, w, 1, 1).astype(BF)
            key_back[rows_h, rows] = (dg(queries, back, 1, 1) * ln2).astype(BF)
            total += jnp.dot(keys[:, rows], back, preferred_element_type=F32)
        query_back[rows_h, :] = (total * (1.0 / math.sqrt(HEAD))).astype(BF)

    @pl.loop(0, HEADS // 2)
    def _(i):
        h = i * 2
        copy_in(h, 0).wait()
        copy_in(h + 1, 1).start()
        head_step(h, 0)
        copy_in(h + 1, 1).wait()

        @pl.when(i < HEADS // 2 - 1)
        def _():
            copy_in(h + 2, 0).start()
        head_step(h + 1, 1)

    @pl.loop(0, SLOT // TILE)
    def _(r):
        rs = rows_at(r * TILE, TILE)
        grad = lower[rs, :]
        grad += dg(query_back[:, rs], w_query[...], 0, 1)
        grad += dg(key_back[:, rs], w_key[...], 0, 1)
        grad += dg(value_back[:, rs], w_value[...], 0, 1)
        input_grad[rs, :] = grad.astype(BF)


def local(tokens, lengths, key_mask, w_query, w_key, w_value, w_output, norm1_gain, norm1_shift,
          w_in, b_in, w_out, norm2_gain, norm2_shift, prefix_key, prefix_value, out_grad):
    rows, width = tokens.shape
    hidden = w_in.shape[1]
    shards = lax.axis_size("mp")
    shape = jax.ShapeDtypeStruct
    params = pltpu.CompilerParams(vmem_limit_bytes=60 * 2**20)

    w_in_all = lax.all_gather(w_in, "mp", axis=0)
    w_out_all = lax.all_gather(w_out, "mp", axis=0)
    b_all = lax.all_gather(jnp.broadcast_to(b_in.astype(F32)[None, :], (8, hidden)), "mp", axis=0)

    square = shape((SLOT, width), BF)
    weights, weights_prefix, query_t, key_t, value, context_t, inverse = pl.pallas_call(
        forward_kernel,
        out_shape=[shape((HEADS, SLOT, SLOT), BF), square, square, square, square, square,
                   shape((HEADS, SLOT), F32)],
        in_specs=[SMEM] + [VMEM] * 7,
        out_specs=[HBM] + [VMEM] * 6,
        scratch_shapes=[
            pltpu.VMEM((SLOT, width), BF),
            pltpu.VMEM((width, SLOT), BF),
            pltpu.VMEM((SLOT, 128), BF),
            pltpu.VMEM((SLOT, SLOT), F32),
            pltpu.VMEM((SLOT, SLOT), F32),
            pltpu.VMEM((HEADS * PREFIX, SLOT), F32),
            pltpu.VMEM((HEADS // GROUP, 8, SLOT), F32),
            pltpu.VMEM((8, SLOT), F32),
            pltpu.VMEM((width, SLOT), F32),
            pltpu.VMEM((HEADS, SLOT), F32),
            pltpu.VMEM((SLOT, SLOT), BF),
            pltpu.VMEM((SLOT, SLOT), BF),
            pltpu.SemaphoreType.DMA((2,)),
        ],
        compiler_params=params,
        name="attend_forward",
    )(lengths, key_mask.reshape(1, SLOT), tokens, w_query, w_key, w_value, prefix_key, prefix_value)

    vectors = jnp.stack([norm1_gain, norm1_shift, norm2_gain, norm2_shift] * 2).astype(F32)
    output, lower, grad_t, centre = pl.pallas_call(
        middle_kernel,
        out_shape=[square, shape((SLOT, width), F32), square, shape((HEADS * 16, SLOT), BF)],
        in_specs=[VMEM] * 9,
        out_specs=[VMEM] * 4,
        scratch_shapes=[
            pltpu.VMEM((SLOT, width), F32),
            pltpu.VMEM((SLOT, 1), F32),
            pltpu.VMEM((SLOT, width), BF),
            pltpu.VMEM((SLOT, width), F32),
            pltpu.VMEM((2, SLOT, hidden), BF),
            pltpu.VMEM((shards, SLOT, hidden), BF),
        ],
        compiler_params=params,
        name="feed_forward",
    )(tokens, context_t, inverse, w_output, vectors, w_in_all, b_all, w_out_all, out_grad)

    input_grad, prefix_grads = pl.pallas_call(
        backward_kernel,
        out_shape=[square, shape((2 * PREFIX, width), F32)],
        in_specs=[HBM] + [VMEM] * 12,
        out_specs=[VMEM] * 2,
        scratch_shapes=[
            pltpu.VMEM((width, SLOT), BF),
            pltpu.VMEM((width, SLOT), BF),
            pltpu.VMEM((width, SLOT), BF),
            pltpu.VMEM((width, SLOT), F32),
            pltpu.VMEM((2, SLOT, SLOT), BF),
            pltpu.SemaphoreType.DMA((2,)),
        ],
        compiler_params=params,
        name="attend_backward",
    )(weights, weights_prefix, query_t, key_t, value, grad_t, centre, prefix_key, prefix_value,
      lower, w_query, w_key, w_value)

    whole = lax.psum(prefix_grads, ("dp", "mp"))
    share = width // shards
    part = lax.dynamic_slice_in_dim(whole, lax.axis_index("mp") * share, share, 1)
    return output, input_grad, part[:PREFIX], part[PREFIX:]


def solution(mesh):
    in_specs = (
        P(("dp", "mp"), None), P(("dp", "mp")), P(("dp", "mp")), P(), P(), P(), P(), P(), P(),
        P(None, "mp"), P("mp"), P("mp", None), P(), P(), P(), P(), P(("dp", "mp"), None),
    )
    out_specs = (P(("dp", "mp"), None), P(("dp", "mp"), None), P(None, "mp"), P(None, "mp"))
    return jax.shard_map(local, mesh=mesh, in_specs=in_specs, out_specs=out_specs, check_vma=False)
```

```python
import functools
import math

import jax
import jax.numpy as jnp
from jax import lax
from jax.experimental import pallas as pl
from jax.experimental.pallas import tpu as pltpu
from jax.sharding import PartitionSpec as P

HEADS = 16
HEAD = 64
PREFIX = 64
SLOT = 1024
GROUP = 4
TILE = 256

EPSILON = 1e-05
MASKED = -1e30
LOG2E = 1.4426950408889634
BF = jnp.bfloat16
F32 = jnp.float32

VMEM = pl.BlockSpec(memory_space=pltpu.VMEM)
SMEM = pl.BlockSpec(memory_space=pltpu.SMEM)
HBM = pl.BlockSpec(memory_space=pl.ANY)


def dg(left, right, left_dim, right_dim):
    return lax.dot_general(
        left, right, (((left_dim,), (right_dim,)), ((), ())), preferred_element_type=F32
    )


def rows_at(start, size):
    return pl.ds(pl.multiple_of(start, size), size)


def block_diagonal(part):
    stacked = jnp.concatenate([part] * GROUP, axis=0)
    head_of_row = lax.broadcasted_iota(jnp.int32, stacked.shape, 0) // HEAD
    head_of_column = lax.broadcasted_iota(jnp.int32, stacked.shape, 1) // HEAD
    return jnp.where(head_of_row == head_of_column, stacked, jnp.zeros_like(stacked))


def diagonal_rows(blocks):
    head_of_row = lax.broadcasted_iota(jnp.int32, blocks.shape, 0) // HEAD
    head_of_column = lax.broadcasted_iota(jnp.int32, blocks.shape, 1) // HEAD
    kept = jnp.where(head_of_row == head_of_column, blocks, jnp.zeros_like(blocks))
    return kept[:64] + kept[64:128] + kept[128:192] + kept[192:]


def ones_rows(width):
    row = lax.broadcasted_iota(jnp.int32, (16, width), 0)
    return jnp.where(row == 0, 1.0, 0.0).astype(BF)


def mask_block(length, mask_ref, mask_cols):
    place = lax.broadcasted_iota(jnp.int32, (1, SLOT), 1)
    live = (place < length) & (mask_ref[...] > 0)
    bias = jnp.where(live, 0.0, MASKED)
    row = lax.broadcasted_iota(jnp.int32, (128, SLOT), 0)
    mask_cols[...] = jnp.where(row == 0, bias, 0.0).T.astype(BF)


MESH = pl.DeviceIdType.MESH
HOPS_IN_LOOP = ((1, (1, 1)), (2, (2, 0)), (3, (1, 2)), (3, (2, 1)), (5, (1, 3)), (5, (2, 2)))
HOPS_AT = {
    "projected": ((1, 0),),
    "attended": ((1, 4), (2, 3)),
    "mixed": ((1, 5), (2, 4)),
    (1, 3): ((1, 6), (2, 5)),
    (2, 1): ((1, 7), (2, 6)),
    (2, 3): ((2, 7),),
}


class Weights:
    def __init__(self, sources, gathered, sems, core_sems, dp, mp, shards):
        self.sources, self.gathered, self.sems, self.core_sems = sources, gathered, sems, core_sems
        self.dp, self.mp = dp, mp
        self.core, self.chip, self.chips = mp % 2, mp // 2, shards // 2
        self.half = dp % 2
        self.chunks = 4 if self.chips <= 2 else 1
        self.beside = (dp + 1 - 2 * (dp % 2), mp)
        self.other = (dp, mp + 1 - 2 * (mp % 2))

    def rows(self, which, half, c):
        size = self.gathered[which].shape[1] // 2
        step = size // self.chunks
        return pl.ds(pl.multiple_of(half * size + c * step, 16), step)

    def shard(self, d, core):
        return ((self.chip - d + self.chips) % self.chips) * 2 + core

    def copy(self, source, target, kind, k, d, device):
        return pltpu.make_async_remote_copy(
            src_ref=source, dst_ref=target, send_sem=self.sems.at[0, kind, k, d],
            recv_sem=self.sems.at[1, kind, k, d], device_id=device, device_id_type=MESH)

    def out_copy(self, k, d):
        which, c = k // self.chunks, k % self.chunks
        rows = self.rows(which, self.half, c)
        target = ((self.chip + d) % self.chips) * 2 + self.core
        return self.copy(self.sources[which].at[rows, :], self.gathered[which].at[self.mp, rows, :], 0, k, d,
                         (self.dp, target))

    def passed(self, kind, k, d, device, core, half):
        which, c = k // self.chunks, k % self.chunks
        place = self.gathered[which].at[self.shard(d, core), self.rows(which, half, c), :]
        return self.copy(place, place, kind, k, d, device)

    def core_copy(self, which):
        return pltpu.make_async_remote_copy(
            src_ref=self.sources[which], dst_ref=self.gathered[which].at[self.mp],
            send_sem=self.core_sems.at[0, which], recv_sem=self.core_sems.at[1, which],
            device_id=self.other, device_id_type=MESH)

    def core_arrival(self, which):
        place = self.gathered[which].at[self.other[1]]
        return pltpu.make_async_remote_copy(
            src_ref=place, dst_ref=place, send_sem=self.core_sems.at[0, which],
            recv_sem=self.core_sems.at[1, which], device_id=self.other, device_id_type=MESH)

    def start(self):
        for k in range(2 * self.chunks):
            for d in range(1, self.chips):
                self.out_copy(k, d).start()
            if k == 1:
                self.core_copy(0).start()
            if k == self.chunks:
                self.core_copy(1).start()

    def first_hop(self, k):
        for d in range(1, self.chips):
            self.passed(0, k, d, self.beside, self.core, self.half).wait_recv()
            self.passed(1, k, d, self.beside, self.core, self.half).start()
            self.passed(2, k, d, self.other, self.core, self.half).start()

    def second_hop(self, k):
        for d in range(1, self.chips):
            self.passed(1, k, d, self.beside, self.core, 1 - self.half).wait_recv()
            self.passed(3, k, d, self.other, self.core, 1 - self.half).start()

    def hops(self, events):
        for kind, k in events:
            if k < 2 * self.chunks:
                (self.first_hop if kind == 1 else self.second_hop)(k)

    def ready(self, which, j):
        d = j // 2
        if j == 1:
            self.core_arrival(which).wait_recv()
        elif j % 2 == 1:
            for c in range(self.chunks):
                k = which * self.chunks + c
                self.passed(2, k, d, self.other, 1 - self.core, self.half).wait_recv()
                self.passed(3, k, d, self.other, 1 - self.core, 1 - self.half).wait_recv()

    def finish(self):
        for k in range(2 * self.chunks):
            for d in range(1, self.chips):
                self.out_copy(k, d).wait_send()
                self.passed(1, k, d, self.beside, self.core, self.half).wait_send()
                self.passed(2, k, d, self.other, self.core, self.half).wait_send()
                self.passed(3, k, d, self.other, self.core, 1 - self.half).wait_send()
        for which in range(2):
            self.core_copy(which).wait_send()


def staged_run(stages, count):
    for step in range(count + len(stages) - 1):
        for s, stage in enumerate(stages):
            if 0 <= step - s < count:
                stage(step - s)


def interleave(*lists):
    for k in range(max(len(parts) for parts in lists)):
        for parts in lists:
            if k < len(parts):
                parts[k]()


def norm_parts(rows):
    centered = rows - jnp.mean(rows, axis=-1, keepdims=True)
    spread = jnp.mean(centered * centered, axis=-1, keepdims=True)
    inverse = lax.rsqrt(spread + EPSILON)
    return centered * inverse, inverse


def norm_back(scaled, unit, inverse):
    first = jnp.mean(scaled, axis=-1, keepdims=True)
    second = jnp.mean(scaled * unit, axis=-1, keepdims=True)
    return inverse * (scaled - first - unit * second)


def gelu_parts(v):
    u = v * (1.0 / math.sqrt(2.0))
    normal = 0.5 * lax.erf(u) + 0.5
    bell = jnp.exp2((u * u) * (-LOG2E))
    return (v * normal).astype(BF), (normal + (u * bell) * (1.0 / math.sqrt(math.pi))).astype(BF)


def layer_kernel(dp_size, shards, length, mask_ref, gain_one, shift_one, gain_two, shift_two, b_in, prefix_key,
                 prefix_value, tokens_hbm, w_query_hbm, w_key_hbm, w_value_hbm, w_output_hbm, w_in_hbm, w_out_hbm,
                 out_grad_hbm, output_hbm, input_grad_hbm, key_share, value_share, kept_hbm,
                 w_in, w_out, bias, pieces, from_group, from_rows, summed, rows_in, query_t, key_t, value, kept_prefix,
                 context_t, w_output, inverse, centre, peaks, prefix_grads,
                 weight_sems, core_sems, bias_sems, group_sems, rows_sems, part_sems, local_sems, keep_sems, out_sems):
    dp, mp = lax.axis_index("dp"), lax.axis_index("mp")
    width = rows_in.shape[1]
    hidden = w_in.shape[2]
    share = width // shards
    blocks = SLOT // TILE
    ln2 = 1.0 / LOG2E
    square = pltpu.VMEM((SLOT, width), BF)
    tall = pltpu.VMEM((SLOT, width), F32)

    barrier = pltpu.get_barrier_semaphore()
    for d in range(1, shards):
        pl.semaphore_signal(barrier, inc=1, device_id=(dp, (mp + d) % shards), device_id_type=MESH)
    for d in range(1, dp_size):
        pl.semaphore_signal(barrier, inc=1, device_id=((dp + d) % dp_size, mp), device_id_type=MESH)

    weights = Weights((w_in_hbm, w_out_hbm), (w_in, w_out), weight_sems, core_sems, dp, mp, shards)

    def remote(source, target, sems, n, device):
        return pltpu.make_async_remote_copy(
            src_ref=source, dst_ref=target, send_sem=sems.at[0, n], recv_sem=sems.at[1, n],
            device_id=device, device_id_type=MESH)

    def load(source, target, n):
        return pltpu.make_async_copy(source, target, local_sems.at[n])

    def group_peer(d):
        return (mp + d) % shards

    def group_sender(d):
        return (mp - d + shards) % shards

    def bias_copy(d):
        return remote(bias.at[mp], bias.at[mp], bias_sems, d, (dp, group_peer(d)))

    def bias_arrival(d):
        place = bias.at[group_sender(d)]
        return remote(place, place, bias_sems, d, (dp, group_peer(d)))

    load(tokens_hbm, rows_in, 0).start()
    own = [load(w_in_hbm, w_in.at[mp], 1), load(w_out_hbm, w_out.at[mp], 2)]
    load_output = load(w_output_hbm, w_output, 3)
    load_grads = load(out_grad_hbm, rows_in, 4)
    store_output = pltpu.make_async_copy(rows_in, output_hbm, out_sems.at[blocks])

    def block(r):
        return slice(r * TILE, (r + 1) * TILE)


    def attention(key, value_t, mask_cols):
        def project(w_query, w_key, w_value):
            def part(n, j):
                cols = rows_at(j * TILE, TILE)
                source = (w_query_hbm, w_key_hbm, w_value_hbm)[n]
                return pltpu.make_async_copy(
                    source.at[:, cols], (w_query, w_key, w_value)[n].at[:, cols], part_sems.at[n, j])

            for j in range(blocks):
                for n in range(3):
                    part(n, j).start()
            for copy in own:
                copy.start()
            load_output.start()
            bias[mp] = jnp.broadcast_to(b_in[...].astype(F32), (8, hidden))
            mask_block(length[0], mask_ref, mask_cols)
            pl.semaphore_wait(barrier, shards - 1 + dp_size - 1)
            weights.start()
            for d in range(1, shards):
                bias_copy(d).start()
            load(tokens_hbm, rows_in, 0).wait()

            @pl.loop(0, blocks)
            def _(j):
                cols = rows_at(j * TILE, TILE)
                part(0, j).wait()
                out = jnp.dot(rows_in[...], w_query[:, cols], preferred_element_type=F32)
                query_t[cols, :] = (out * (LOG2E / math.sqrt(HEAD))).astype(BF).T
                part(1, j).wait()
                out = jnp.dot(rows_in[...], w_key[:, cols], preferred_element_type=F32).astype(BF)
                key[:, cols] = out
                key_t[cols, :] = out.T
                part(2, j).wait()
                out = jnp.dot(rows_in[...], w_value[:, cols], preferred_element_type=F32).astype(BF)
                value[:, cols] = out
                value_t[cols, :] = out.T

        pl.run_scoped(project, *[pltpu.VMEM((width, width), BF)] * 3)
        weights.hops(HOPS_AT["projected"])
        long = pltpu.VMEM((SLOT + PREFIX, SLOT), F32)
        kept = pltpu.VMEM((SLOT, SLOT), BF)
        pl.run_scoped(functools.partial(attend, key, value_t, mask_cols), long, long, kept, kept,
                      pltpu.VMEM((2 * HEAD, SLOT), F32), pltpu.VMEM((8, SLOT), F32))

    def attend(key, value_t, mask_cols, scores_a, scores_b, kept_a, kept_b, sums, totals):
        prefix_rows = slice(SLOT, SLOT + PREFIX)

        def right_side(h, half):
            q = query_t[rows_at(h * HEAD, HEAD), :]
            zero = jnp.zeros_like(q)
            last = jnp.concatenate([ones_rows(SLOT), jnp.zeros((112, SLOT), BF)], axis=0)
            return jnp.concatenate([q, zero, last] if half == 0 else [zero, q, last], axis=0)

        def folded(s):
            return jnp.max(s.reshape(s.shape[0] // 8, 8, SLOT), axis=0)

        def score_tile(h, t, right, scores, peak):
            rows = block(t)
            pair = rows_at((h // 2) * 128, 128)
            left = jnp.concatenate([key[rows, pair], mask_cols[rows, :]], axis=1)
            s = jnp.dot(left, right, preferred_element_type=F32)
            scores[rows, :] = s
            peak = folded(s) if peak is None else jnp.maximum(peak, folded(s))
            if t == blocks - 1:
                left = jnp.concatenate([prefix_key[:, pair], jnp.zeros((PREFIX, 128), BF)], axis=1)
                s = jnp.dot(left, right, preferred_element_type=F32)
                scores[prefix_rows, :] = s
                peak = jnp.maximum(peak, folded(s))
            return peak

        def set_peak(half, peak):
            peaks[half : half + 1, :] = jnp.max(peak, axis=0, keepdims=True)

        def head_step(h, half, scores_new, scores_old, kept, more):
            if more:
                right = right_side(h + 1, 1 - half)
            top = peaks[half : half + 1, :]
            rows_h = rows_at(h * HEAD, HEAD)
            left = jnp.concatenate([value_t[rows_h, :], ones_rows(SLOT)], axis=0)
            total = jnp.zeros((80, SLOT), F32)
            peak = None
            for t in range(blocks):
                rows = block(t)
                if more:
                    peak = score_tile(h + 1, t, right, scores_new, peak)
                p = jnp.exp2(scores_old[rows, :] - top).astype(BF)
                kept[rows, :] = p
                total += jnp.dot(left[:, rows], p, preferred_element_type=F32)
            kept_prefix[rows_h, :] = jnp.exp2(scores_old[prefix_rows, :] - top).astype(BF)
            if more:
                set_peak(1 - half, peak)
            sums[half * HEAD : (half + 1) * HEAD, :] = total[:HEAD]
            totals[half : half + 1, :] = total[HEAD : HEAD + 1]

        def finish_pair(i):
            pair = rows_at(i * 128, 128)
            row = lax.broadcasted_iota(jnp.int32, (128, 256), 0) // HEAD
            column = lax.broadcasted_iota(jnp.int32, (128, 256), 1)
            part = prefix_value[:, pair]
            both = jnp.concatenate([part, part], axis=0)
            both = jnp.concatenate([both, jnp.ones((128, 128), BF)], axis=1)
            wanted = jnp.where(column < 128, column // HEAD, column - 128)
            left = jnp.where(row == wanted, both, jnp.zeros_like(both))
            extra = dg(left, kept_prefix[pair, :], 0, 0)
            for n in range(2):
                scale = 1.0 / (totals[n : n + 1, :] + extra[128 + n : 129 + n, :])
                inverse[pl.ds(2 * i + n, 1), :] = scale
                own_rows = slice(n * HEAD, (n + 1) * HEAD)
                context_t[rows_at((2 * i + n) * HEAD, HEAD), :] = (
                    (sums[own_rows, :] + extra[own_rows, :]) * scale
                ).astype(BF)

        def keep(h, half):
            return pltpu.make_async_copy((kept_a, kept_b)[half], kept_hbm.at[h], keep_sems.at[half])

        right = right_side(0, 0)
        peak = None
        for t in range(blocks):
            peak = score_tile(0, t, right, scores_a, peak)
        set_peak(0, peak)

        @pl.loop(0, HEADS // 2 - 1)
        def _(i):
            h = i * 2

            @pl.when(i > 0)
            def _():
                keep(h - 2, 0).wait()
            head_step(h, 0, scores_b, scores_a, kept_a, True)
            keep(h, 0).start()

            @pl.when(i > 0)
            def _():
                keep(h - 1, 1).wait()
            head_step(h + 1, 1, scores_a, scores_b, kept_b, True)
            keep(h + 1, 1).start()
            finish_pair(i)
            for n, event in HOPS_IN_LOOP:
                @pl.when(i == n)
                def _():
                    weights.hops((event,))

        h = HEADS - 2
        keep(h - 2, 0).wait()
        head_step(h, 0, scores_b, scores_a, kept_a, True)
        keep(h, 0).start()
        keep(h - 1, 1).wait()
        head_step(h + 1, 1, scores_a, scores_b, kept_b, False)
        keep(h + 1, 1).start()
        finish_pair(HEADS // 2 - 1)
        keep(h, 0).wait()
        keep(h + 1, 1).wait()

    pl.run_scoped(attention, square, square, pltpu.VMEM((SLOT, 128), BF))
    weights.hops(HOPS_AT["attended"])


    def feed_forward(unit, inverse_one, low, active, slope):
        gain_1, shift_1 = gain_one[...].astype(F32), shift_one[...].astype(F32)
        gain_2, shift_2 = gain_two[...].astype(F32), shift_two[...].astype(F32)
        everything = slice(0, SLOT)

        def shard_at(j):
            return weights.shard(j // 2, (weights.core + j) % 2)

        def mix(r):
            rs = block(r)
            summed[rs, :] = rows_in[rs, :].astype(F32) + dg(context_t[:, rs], w_output[...], 0, 0)

        def norm_one(r):
            rs = block(r)
            u, inv = norm_parts(summed[rs, :])
            unit[rs, :] = u
            inverse_one[rs, :] = inv
            normed = u * gain_1 + shift_1
            summed[rs, :] = normed
            low[rs, :] = normed.astype(BF)

        def first(j, rs, cols):
            s = shard_at(j)
            pre = jnp.dot(low[rs, :], w_in[s, :, cols], preferred_element_type=F32) + bias[s, 0:1, cols]
            act, slo = gelu_parts(pre)
            active[j % 2, rs, cols] = act
            slope[j, rs, cols] = slo

        def second(j, rs, cols):
            summed[rs, cols] += jnp.dot(active[j % 2, rs, :], w_out[shard_at(j), :, cols], preferred_element_type=F32)

        def norm_two(r):
            rs = block(r)
            u, inv = norm_parts(summed[rs, :])
            upper = norm_back(rows_in[rs, :].astype(F32) * gain_2, u, inv)
            rows_in[rs, :] = (u * gain_2 + shift_2).astype(BF)
            summed[rs, :] = upper
            low[rs, :] = upper.astype(BF)

        def third(j, rs, cols):
            grad = dg(low[rs, :], w_out[shard_at(j), cols, :], 1, 1)
            active[j % 2, rs, cols] = (grad * slope[j, rs, cols].astype(F32)).astype(BF)

        def fourth(j, rs, cols):
            summed[rs, cols] += dg(active[j % 2, rs, :], w_in[shard_at(j), cols, :], 1, 1)

        def norm_one_back(r):
            rs = block(r)
            grad = norm_back(summed[rs, :] * gain_1, unit[rs, :], inverse_one[rs, :])
            summed[rs, :] = grad
            low[rs, :] = grad.astype(BF)

        def parts(function, j, size):
            return [functools.partial(function, j, everything, slice(c, c + TILE)) for c in range(0, size, TILE)]

        def hops(j):
            return [functools.partial(weights.hops, HOPS_AT.get((j, n), ())) for n in range(width // TILE)]

        load_output.wait()
        own[0].wait()
        staged_run([mix, norm_one, lambda r: first(0, block(r), slice(0, hidden))], blocks)
        load_grads.start()
        weights.hops(HOPS_AT["mixed"])
        for d in range(1, shards):
            bias_arrival(d).wait_recv()
        own[1].wait()
        for j in range(1, shards):
            weights.ready(0, j)
            weights.ready(1, j - 1)
            interleave(parts(first, j, hidden), parts(second, j - 1, width), hops(j))
        last = shards - 1
        weights.ready(1, last)
        load_grads.wait()

        whole = slice(0, width)
        staged_run([lambda r: second(last, block(r), whole), norm_two,
                    lambda r: third(0, block(r), slice(0, hidden))], blocks)
        store_output.start()
        for j in range(1, shards):
            interleave(parts(third, j, hidden), parts(fourth, j - 1, width))
        staged_run([lambda r: fourth(last, block(r), whole), norm_one_back], blocks)

        @pl.loop(0, width // TILE)
        def _(g):
            grad = dg(w_output[rows_at(g * TILE, TILE), :], low[...], 1, 1)
            row = lax.broadcasted_iota(jnp.int32, (16, SLOT), 0)
            for i in range(TILE // HEAD):
                h = g * (TILE // HEAD) + i
                rows_h = rows_at(h * HEAD, HEAD)
                scaled = grad[i * HEAD : (i + 1) * HEAD] * inverse[pl.ds(h, 1), :]
                middle = -jnp.sum(scaled * context_t[rows_h, :].astype(F32), axis=0, keepdims=True)
                context_t[rows_h, :] = scaled.astype(BF)
                high = middle.astype(BF).astype(F32)
                both = jnp.where(row == 0, high, jnp.where(row == 1, middle - high, 0.0))
                centre[rows_at(h * 16, 16), :] = both.astype(BF)

    pl.run_scoped(feed_forward, tall, pltpu.VMEM((SLOT, 1), F32), square,
                  pltpu.VMEM((2, SLOT, hidden), BF), pltpu.VMEM((shards, SLOT, hidden), BF))
    weights.finish()
    for d in range(1, shards):
        bias_copy(d).wait_send()


    grad_t = context_t

    def group_copy(d):
        return remote(pieces.at[group_peer(d)], from_group.at[mp], group_sems, d, (dp, group_peer(d)))

    def group_arrival(d):
        place = from_group.at[group_sender(d)]
        return remote(place, place, group_sems, d, (dp, group_peer(d)))

    def rows_copy(d):
        return remote(from_rows.at[dp], from_rows.at[dp], rows_sems, d, ((dp + d) % dp_size, mp))

    def rows_arrival(d):
        place = from_rows.at[(dp - d + dp_size) % dp_size]
        return remote(place, place, rows_sems, d, ((dp + d) % dp_size, mp))

    def attend_back(query_back, key_back, value_back, query_prefix, staged, w_query, w_key, w_value):
        loads = [load(w_query_hbm, w_query, 5), load(w_key_hbm, w_key, 6), load(w_value_hbm, w_value, 7)]

        def copy_in(h, half):
            return pltpu.make_async_copy(kept_hbm.at[h], staged.at[half], keep_sems.at[half])

        copy_in(0, 0).start()
        for copy in loads:
            copy.start()

        @pl.loop(0, HEADS // GROUP)
        def _(g):
            cols = rows_at(g * 256, 256)
            grads = grad_t[cols, :]
            back = jnp.dot(block_diagonal(prefix_value[:, cols]), grads, preferred_element_type=F32)
            parts = []
            for i in range(GROUP):
                h = g * GROUP + i
                middle = jnp.sum(centre[rows_at(h * 16, 16), :].astype(F32), axis=0, keepdims=True)
                kept = kept_prefix[rows_at(h * HEAD, HEAD), :].astype(F32)
                parts.append((kept * (back[i * HEAD : (i + 1) * HEAD] + middle)).astype(BF))
            back = jnp.concatenate(parts, axis=0)
            prefix_grads[:PREFIX, cols] = diagonal_rows(dg(back, query_t[cols, :], 1, 1)) * ln2
            prefix_grads[PREFIX:, cols] = diagonal_rows(dg(kept_prefix[cols, :], grads, 1, 1))
            query_prefix[cols, :] = dg(block_diagonal(prefix_key[:, cols]), back, 0, 0)

        for s in range(shards):
            pieces[s] = prefix_grads[:, s * share : (s + 1) * share]
        for d in range(1, shards):
            group_copy(d).start()

        lane = lax.broadcasted_iota(jnp.int32, (TILE, 128), 1)
        pick = jnp.where(lane < 2, 1.0, 0.0).astype(BF)

        def head_step(h, half):
            rows_h = rows_at(h * HEAD, HEAD)
            pair = rows_at((h // 2) * 128, 128)
            grads = grad_t[rows_h, :]
            zero = jnp.zeros_like(grads)
            last = jnp.concatenate([centre[rows_at(h * 16, 16), :], jnp.zeros((112, SLOT), BF)], axis=0)
            right = jnp.concatenate([grads, zero, last] if half == 0 else [zero, grads, last], axis=0)
            queries = query_t[rows_h, :]
            keys = key_t[rows_h, :]
            total = query_prefix[rows_h, :]
            for t in range(blocks):
                rows = block(t)
                left = jnp.concatenate([value[rows, pair], pick], axis=1)
                back = jnp.dot(left, right, preferred_element_type=F32)
                w = staged[half, rows, :]
                back = (back * w.astype(F32)).astype(BF)
                value_back[rows_h, rows] = dg(grads, w, 1, 1).astype(BF)
                key_back[rows_h, rows] = (dg(queries, back, 1, 1) * ln2).astype(BF)
                total += jnp.dot(keys[:, rows], back, preferred_element_type=F32)
            query_back[rows_h, :] = (total * (1.0 / math.sqrt(HEAD))).astype(BF)

        @pl.loop(0, HEADS // 2)
        def _(i):
            h = i * 2
            copy_in(h, 0).wait()
            copy_in(h + 1, 1).start()
            head_step(h, 0)
            copy_in(h + 1, 1).wait()

            @pl.when(i < HEADS // 2 - 1)
            def _():
                copy_in(h + 2, 0).start()
            head_step(h + 1, 1)

            @pl.when(i == 1)
            def _():
                own_piece = pieces[mp]
                for d in range(1, shards):
                    group_arrival(d).wait_recv()
                    own_piece += from_group[group_sender(d)]
                from_rows[dp] = own_piece
                for d in range(1, dp_size):
                    rows_copy(d).start()

        store_output.wait()
        for copy in loads:
            copy.wait()
        result = rows_in

        def store(r):
            rs = rows_at(r * TILE, TILE)
            return pltpu.make_async_copy(result.at[rs, :], input_grad_hbm.at[rs, :], out_sems.at[r])

        @pl.loop(0, blocks)
        def _(r):
            rs = rows_at(r * TILE, TILE)
            grad = summed[rs, :]
            grad += dg(query_back[:, rs], w_query[...], 0, 1)
            grad += dg(key_back[:, rs], w_key[...], 0, 1)
            grad += dg(value_back[:, rs], w_value[...], 0, 1)
            result[rs, :] = grad.astype(BF)
            store(r).start()

        for d in range(1, dp_size):
            rows_arrival(d).wait_recv()
        total = from_rows[0]
        for n in range(1, dp_size):
            total += from_rows[n]
        key_share[...] = total[:PREFIX]
        value_share[...] = total[PREFIX:]
        for d in range(1, shards):
            group_copy(d).wait_send()
        for d in range(1, dp_size):
            rows_copy(d).wait_send()
        for r in range(blocks):
            store(r).wait()

    pl.run_scoped(attend_back, square, square, square, tall, pltpu.VMEM((2, SLOT, SLOT), BF),
                  *[pltpu.VMEM((width, width), BF)] * 3)


def local(dp_size, shards, tokens, lengths, key_mask, w_query, w_key, w_value, w_output, norm1_gain, norm1_shift,
          w_in, b_in, w_out, norm2_gain, norm2_shift, prefix_key, prefix_value, out_grad):
    rows, width = tokens.shape
    hidden = w_in.shape[1]
    share = width // shards
    chips = shards // 2
    shape = jax.ShapeDtypeStruct
    square = pltpu.VMEM((SLOT, width), BF)
    dma = pltpu.SemaphoreType.DMA
    line = (1, width)
    output, input_grad, key_grad, value_grad, _ = pl.pallas_call(
        functools.partial(layer_kernel, dp_size, shards),
        out_shape=[shape((rows, width), BF), shape((rows, width), BF), shape((PREFIX, share), F32),
                   shape((PREFIX, share), F32), shape((HEADS, SLOT, SLOT), BF)],
        in_specs=[SMEM] + [VMEM] * 8 + [HBM] * 8,
        out_specs=[HBM, HBM, VMEM, VMEM, HBM],
        scratch_shapes=[
            pltpu.VMEM((shards, width, hidden), BF),
            pltpu.VMEM((shards, hidden, width), BF),
            pltpu.VMEM((shards, 8, hidden), F32),
            pltpu.VMEM((shards, 2 * PREFIX, share), F32),
            pltpu.VMEM((shards, 2 * PREFIX, share), F32),
            pltpu.VMEM((dp_size, 2 * PREFIX, share), F32),
            pltpu.VMEM((SLOT, width), F32),
            square, square, square, square, square, square, square,
            pltpu.VMEM((HEADS, SLOT), F32),
            pltpu.VMEM((HEADS * 16, SLOT), BF),
            pltpu.VMEM((8, SLOT), F32),
            pltpu.VMEM((2 * PREFIX, width), F32),
            dma((2, 4, 8 if chips <= 2 else 2, max(chips, 2))),
            dma((2, 2)),
            dma((2, shards)),
            dma((2, shards)),
            dma((2, dp_size)),
            dma((3, SLOT // TILE)),
            dma((8,)),
            dma((2,)),
            dma((SLOT // TILE + 1,)),
        ],
        compiler_params=pltpu.CompilerParams(
            vmem_limit_bytes=61 * 2**20, collective_id=0, has_side_effects=True),
        cost_estimate=pl.CostEstimate(flops=70 * 10**9, bytes_accessed=10**8, transcendentals=3 * 10**7),
        name="layer",
    )(lengths, key_mask.reshape(1, SLOT), norm1_gain.reshape(line), norm1_shift.reshape(line),
      norm2_gain.reshape(line), norm2_shift.reshape(line), b_in.reshape(1, hidden), prefix_key, prefix_value,
      tokens, w_query, w_key, w_value, w_output, w_in, w_out, out_grad)
    return output, input_grad, key_grad, value_grad


def solution(mesh):
    in_specs = (
        P(("dp", "mp"), None), P(("dp", "mp")), P(("dp", "mp")), P(), P(), P(), P(), P(), P(),
        P(None, "mp"), P("mp"), P("mp", None), P(), P(), P(), P(), P(("dp", "mp"), None),
    )
    out_specs = (P(("dp", "mp"), None), P(("dp", "mp"), None), P(None, "mp"), P(None, "mp"))
    return jax.shard_map(
        functools.partial(local, mesh.shape["dp"], mesh.shape["mp"]),
        mesh=mesh, in_specs=in_specs, out_specs=out_specs, check_vma=False)
```

```python
import functools
import math

import jax
import jax.numpy as jnp
from jax import lax
from jax.experimental import pallas as pl
from jax.experimental.pallas import tpu as pltpu
from jax.sharding import PartitionSpec as P

HEADS = 16
HEAD = 64
PREFIX = 64
SLOT = 1024
GROUP = 4
TILE = 256

EPSILON = 1e-05
MASKED = -1e30
LOG2E = 1.4426950408889634
BF = jnp.bfloat16
F32 = jnp.float32

VMEM = pl.BlockSpec(memory_space=pltpu.VMEM)
SMEM = pl.BlockSpec(memory_space=pltpu.SMEM)
HBM = pl.BlockSpec(memory_space=pl.ANY)


def dg(left, right, left_dim, right_dim):
    return lax.dot_general(
        left, right, (((left_dim,), (right_dim,)), ((), ())), preferred_element_type=F32
    )


def rows_at(start, size):
    return pl.ds(pl.multiple_of(start, size), size)


def block_diagonal(part):
    stacked = jnp.concatenate([part] * GROUP, axis=0)
    head_of_row = lax.broadcasted_iota(jnp.int32, stacked.shape, 0) // HEAD
    head_of_column = lax.broadcasted_iota(jnp.int32, stacked.shape, 1) // HEAD
    return jnp.where(head_of_row == head_of_column, stacked, jnp.zeros_like(stacked))


def diagonal_rows(blocks):
    head_of_row = lax.broadcasted_iota(jnp.int32, blocks.shape, 0) // HEAD
    head_of_column = lax.broadcasted_iota(jnp.int32, blocks.shape, 1) // HEAD
    kept = jnp.where(head_of_row == head_of_column, blocks, jnp.zeros_like(blocks))
    return kept[:64] + kept[64:128] + kept[128:192] + kept[192:]


def ones_rows(width):
    row = lax.broadcasted_iota(jnp.int32, (16, width), 0)
    return jnp.where(row == 0, 1.0, 0.0).astype(BF)


def mask_block(length, mask_ref, mask_cols):
    place = lax.broadcasted_iota(jnp.int32, (1, SLOT), 1)
    live = (place < length) & (mask_ref[...] > 0)
    bias = jnp.where(live, 0.0, MASKED)
    row = lax.broadcasted_iota(jnp.int32, (128, SLOT), 0)
    mask_cols[...] = jnp.where(row == 0, bias, 0.0).T.astype(BF)


MESH = pl.DeviceIdType.MESH
HOPS_IN_LOOP = ((0, ("y", 0)), (2, ("y", 1)), (3, ("x", 0)), (3, ("z", 0)), (4, ("y", 2)), (6, ("x", 1)))
HOPS_AT = {
    "attended": (("y", 3), ("z", 1)),
    ("mix", 2): (("x", 2),),
    ("mix", 4): (("z", 2),),
    ("mix", 5): (("d", 0),),
    (1, 0): (("x", 3),),
    (1, 1): (("z", 3), ("d", 1)),
    (1, 3): (("d", 2),),
    (2, 3): (("d", 3),),
}


class Weights:
    def __init__(self, sources, gathered, sems, core_sems, dp, mp, shards):
        self.sources, self.gathered, self.sems, self.core_sems = sources, gathered, sems, core_sems
        self.dp, self.mp = dp, mp
        self.core, self.chip, self.chips = mp % 2, mp // 2, shards // 2
        self.a, self.b = dp % 2, (dp // 2) % 2
        self.chunks = 2 if self.chips <= 2 else 1
        self.beside_x = (dp + 1 - 2 * self.a, mp)
        self.beside_z = (dp + 2 - 4 * self.b, mp)
        self.other = (dp, mp + 1 - 2 * (mp % 2))
        self.own_quarter = (self.a, self.b)
        self.x_quarter = (1 - self.a, self.b)
        self.z_quarter = (self.a, 1 - self.b)
        self.far_quarter = (1 - self.a, 1 - self.b)

    def rows(self, which, quarter, c):
        size = self.gathered[which].shape[1] // 4
        step = size // self.chunks
        return pl.ds(pl.multiple_of((quarter[0] * 2 + quarter[1]) * size + c * step, 16), step)

    def shard(self, d, core):
        return ((self.chip - d + self.chips) % self.chips) * 2 + core

    def copy(self, source, target, kind, k, d, device):
        return pltpu.make_async_remote_copy(
            src_ref=source, dst_ref=target, send_sem=self.sems.at[0, kind, k, d],
            recv_sem=self.sems.at[1, kind, k, d], device_id=device, device_id_type=MESH)

    def out_copy(self, k, d):
        which, c = k // self.chunks, k % self.chunks
        rows = self.rows(which, self.own_quarter, c)
        target = ((self.chip + d) % self.chips) * 2 + self.core
        return self.copy(self.sources[which].at[rows, :], self.gathered[which].at[self.mp, rows, :], 0, k, d,
                         (self.dp, target))

    def passed(self, kind, k, d, quarter, device, core=None):
        which, c = k // self.chunks, k % self.chunks
        shard = self.shard(d, self.core if core is None else core)
        place = self.gathered[which].at[shard, self.rows(which, quarter, c), :]
        return self.copy(place, place, kind, k, d, device)

    def across(self, k, d):
        if k % self.chunks == 0:
            return self.passed(3, k, d, self.x_quarter, self.beside_z)
        return self.passed(3, k, d, self.z_quarter, self.beside_x)

    def core_copy(self, which):
        return pltpu.make_async_remote_copy(
            src_ref=self.sources[which], dst_ref=self.gathered[which].at[self.mp],
            send_sem=self.core_sems.at[0, which], recv_sem=self.core_sems.at[1, which],
            device_id=self.other, device_id_type=MESH)

    def core_arrival(self, which):
        place = self.gathered[which].at[self.other[1]]
        return pltpu.make_async_remote_copy(
            src_ref=place, dst_ref=place, send_sem=self.core_sems.at[0, which],
            recv_sem=self.core_sems.at[1, which], device_id=self.other, device_id_type=MESH)

    def start(self):
        for k in range(2 * self.chunks):
            for d in range(1, self.chips):
                self.out_copy(k, d).start()
        for which in range(2):
            self.core_copy(which).start()

    def arrival(self, event, k, d):
        kind, quarter = {"y": (0, self.own_quarter), "x": (1, self.x_quarter), "z": (2, self.z_quarter),
                         "d": (3, self.far_quarter)}[event]
        return self.passed(kind, k, d, quarter, self.other)

    def onward(self, event, k, d):
        if event == "y":
            return [self.passed(1, k, d, self.own_quarter, self.beside_x),
                    self.passed(2, k, d, self.own_quarter, self.beside_z),
                    self.passed(4, k, d, self.own_quarter, self.other)]
        if event == "d":
            return [self.passed(7, k, d, self.far_quarter, self.other)]
        copies = [self.passed(5, k, d, self.x_quarter, self.other) if event == "x"
                  else self.passed(6, k, d, self.z_quarter, self.other)]
        if (k % self.chunks == 0) == (event == "x"):
            copies.append(self.across(k, d))
        return copies

    def hops(self, events):
        for event, k in events:
            if k < 2 * self.chunks:
                for d in range(1, self.chips):
                    self.arrival(event, k, d).wait_recv()
                    for copy in self.onward(event, k, d):
                        copy.start()

    def ready(self, which, j):
        d = j // 2
        if j == 1:
            self.core_arrival(which).wait_recv()
        elif j % 2 == 1:
            for c in range(self.chunks):
                k = which * self.chunks + c
                for kind, quarter in ((4, self.own_quarter), (5, self.x_quarter), (6, self.z_quarter),
                                      (7, self.far_quarter)):
                    self.passed(kind, k, d, quarter, self.other, 1 - self.core).wait_recv()

    def finish(self):
        for k in range(2 * self.chunks):
            for d in range(1, self.chips):
                self.out_copy(k, d).wait_send()
                for event in "yxzd":
                    for copy in self.onward(event, k, d):
                        copy.wait_send()
        for which in range(2):
            self.core_copy(which).wait_send()


def staged_run(stages, count, after=None):
    for step in range(count + len(stages) - 1):
        for s, stage in enumerate(stages):
            if 0 <= step - s < count:
                stage(step - s)
        if after is not None:
            after(step)


def interleave(*lists):
    for k in range(max(len(parts) for parts in lists)):
        for parts in lists:
            if k < len(parts):
                parts[k]()


def norm_parts(rows):
    centered = rows - jnp.mean(rows, axis=-1, keepdims=True)
    spread = jnp.mean(centered * centered, axis=-1, keepdims=True)
    inverse = lax.rsqrt(spread + EPSILON)
    return centered * inverse, inverse


def norm_back(scaled, unit, inverse):
    first = jnp.mean(scaled, axis=-1, keepdims=True)
    second = jnp.mean(scaled * unit, axis=-1, keepdims=True)
    return inverse * (scaled - first - unit * second)


def gelu_parts(v):
    u = v * (1.0 / math.sqrt(2.0))
    normal = 0.5 * lax.erf(u) + 0.5
    bell = jnp.exp2((u * u) * (-LOG2E))
    return (v * normal).astype(BF), (normal + (u * bell) * (1.0 / math.sqrt(math.pi))).astype(BF)


def layer_kernel(dp_size, shards, length, mask_ref, gain_one, shift_one, gain_two, shift_two, b_in, prefix_key,
                 prefix_value, tokens_hbm, w_query_hbm, w_key_hbm, w_value_hbm, w_output_hbm, w_in_hbm, w_out_hbm,
                 out_grad_hbm, output_hbm, input_grad_hbm, key_share, value_share, kept_hbm,
                 w_in, w_out, bias, pieces, from_group, from_rows, summed, rows_in, query_t, key_t, value, kept_prefix,
                 context_t, w_output, inverse, centre, peaks, prefix_grads,
                 weight_sems, core_sems, bias_sems, group_sems, rows_sems, part_sems, local_sems, keep_sems, out_sems):
    dp, mp = lax.axis_index("dp"), lax.axis_index("mp")
    width = rows_in.shape[1]
    hidden = w_in.shape[2]
    share = width // shards
    blocks = SLOT // TILE
    ln2 = 1.0 / LOG2E
    square = pltpu.VMEM((SLOT, width), BF)
    tall = pltpu.VMEM((SLOT, width), F32)

    barrier = pltpu.get_barrier_semaphore()
    for d in range(1, shards):
        pl.semaphore_signal(barrier, inc=1, device_id=(dp, (mp + d) % shards), device_id_type=MESH)
    for d in range(1, dp_size):
        pl.semaphore_signal(barrier, inc=1, device_id=((dp + d) % dp_size, mp), device_id_type=MESH)

    weights = Weights((w_in_hbm, w_out_hbm), (w_in, w_out), weight_sems, core_sems, dp, mp, shards)

    def remote(source, target, sems, n, device):
        return pltpu.make_async_remote_copy(
            src_ref=source, dst_ref=target, send_sem=sems.at[0, n], recv_sem=sems.at[1, n],
            device_id=device, device_id_type=MESH)

    def load(source, target, n):
        return pltpu.make_async_copy(source, target, local_sems.at[n])

    def group_peer(d):
        return (mp + d) % shards

    def group_sender(d):
        return (mp - d + shards) % shards

    def bias_copy(d):
        return remote(bias.at[mp], bias.at[mp], bias_sems, d, (dp, group_peer(d)))

    def bias_arrival(d):
        place = bias.at[group_sender(d)]
        return remote(place, place, bias_sems, d, (dp, group_peer(d)))

    load(tokens_hbm, rows_in, 0).start()
    own = [load(w_in_hbm, w_in.at[mp], 1), load(w_out_hbm, w_out.at[mp], 2)]
    load_output = load(w_output_hbm, w_output, 3)
    load_grads = load(out_grad_hbm, rows_in, 4)
    store_output = pltpu.make_async_copy(rows_in, output_hbm, out_sems.at[blocks])

    def block(r):
        return slice(r * TILE, (r + 1) * TILE)


    def attention(key, value_t, mask_cols):
        def project(w_query, w_key, w_value):
            def part(n, j):
                cols = rows_at(j * TILE, TILE)
                source = (w_query_hbm, w_key_hbm, w_value_hbm)[n]
                return pltpu.make_async_copy(
                    source.at[:, cols], (w_query, w_key, w_value)[n].at[:, cols], part_sems.at[n, j])

            for j in range(blocks):
                for n in range(3):
                    part(n, j).start()
            for copy in own:
                copy.start()
            load_output.start()
            bias[mp] = jnp.broadcast_to(b_in[...].astype(F32)[None, :], (8, hidden))
            mask_block(length[0], mask_ref, mask_cols)
            load(tokens_hbm, rows_in, 0).wait()

            def columns(j):
                cols = rows_at(j * TILE, TILE)
                part(0, j).wait()
                out = jnp.dot(rows_in[...], w_query[:, cols], preferred_element_type=F32)
                query_t[cols, :] = (out * (LOG2E / math.sqrt(HEAD))).astype(BF).T
                part(1, j).wait()
                out = jnp.dot(rows_in[...], w_key[:, cols], preferred_element_type=F32).astype(BF)
                key[:, cols] = out
                key_t[cols, :] = out.T
                part(2, j).wait()
                out = jnp.dot(rows_in[...], w_value[:, cols], preferred_element_type=F32).astype(BF)
                value[:, cols] = out
                value_t[cols, :] = out.T

            pl.loop(0, 1)(columns)
            pl.semaphore_wait(barrier, shards - 1 + dp_size - 1)
            weights.start()
            for d in range(1, shards):
                bias_copy(d).start()
            pl.loop(1, blocks)(columns)

        pl.run_scoped(project, *[pltpu.VMEM((width, width), BF)] * 3)
        long = pltpu.VMEM((SLOT + PREFIX, SLOT), F32)
        kept = pltpu.VMEM((SLOT, SLOT), BF)
        pl.run_scoped(functools.partial(attend, key, value_t, mask_cols), long, long, kept, kept,
                      pltpu.VMEM((2 * HEAD, SLOT), F32), pltpu.VMEM((8, SLOT), F32))

    def attend(key, value_t, mask_cols, scores_a, scores_b, kept_a, kept_b, sums, totals):
        prefix_rows = slice(SLOT, SLOT + PREFIX)

        def right_side(h, half):
            q = query_t[rows_at(h * HEAD, HEAD), :]
            zero = jnp.zeros_like(q)
            last = jnp.concatenate([ones_rows(SLOT), jnp.zeros((112, SLOT), BF)], axis=0)
            return jnp.concatenate([q, zero, last] if half == 0 else [zero, q, last], axis=0)

        def folded(s):
            return jnp.max(s.reshape(s.shape[0] // 8, 8, SLOT), axis=0)

        def score_tile(h, t, right, scores, peak):
            rows = block(t)
            pair = rows_at((h // 2) * 128, 128)
            left = jnp.concatenate([key[rows, pair], mask_cols[rows, :]], axis=1)
            s = jnp.dot(left, right, preferred_element_type=F32)
            scores[rows, :] = s
            peak = folded(s) if peak is None else jnp.maximum(peak, folded(s))
            if t == blocks - 1:
                left = jnp.concatenate([prefix_key[:, pair], jnp.zeros((PREFIX, 128), BF)], axis=1)
                s = jnp.dot(left, right, preferred_element_type=F32)
                scores[prefix_rows, :] = s
                peak = jnp.maximum(peak, folded(s))
            return peak

        def set_peak(half, peak):
            peaks[half : half + 1, :] = jnp.max(peak, axis=0, keepdims=True)

        def head_step(h, half, scores_new, scores_old, kept, more):
            if more:
                right = right_side(h + 1, 1 - half)
            top = peaks[half : half + 1, :]
            rows_h = rows_at(h * HEAD, HEAD)
            left = jnp.concatenate([value_t[rows_h, :], ones_rows(SLOT)], axis=0)
            total = jnp.zeros((80, SLOT), F32)
            peak = None
            for t in range(blocks):
                rows = block(t)
                if more:
                    peak = score_tile(h + 1, t, right, scores_new, peak)
                p = jnp.exp2(scores_old[rows, :] - top).astype(BF)
                kept[rows, :] = p
                total += jnp.dot(left[:, rows], p, preferred_element_type=F32)
            kept_prefix[rows_h, :] = jnp.exp2(scores_old[prefix_rows, :] - top).astype(BF)
            if more:
                set_peak(1 - half, peak)
            sums[half * HEAD : (half + 1) * HEAD, :] = total[:HEAD]
            totals[half : half + 1, :] = total[HEAD : HEAD + 1]

        def finish_pair(i):
            pair = rows_at(i * 128, 128)
            row = lax.broadcasted_iota(jnp.int32, (128, 256), 0) // HEAD
            column = lax.broadcasted_iota(jnp.int32, (128, 256), 1)
            part = prefix_value[:, pair]
            both = jnp.concatenate([part, part], axis=0)
            both = jnp.concatenate([both, jnp.ones((128, 128), BF)], axis=1)
            wanted = jnp.where(column < 128, column // HEAD, column - 128)
            left = jnp.where(row == wanted, both, jnp.zeros_like(both))
            extra = dg(left, kept_prefix[pair, :], 0, 0)
            for n in range(2):
                scale = 1.0 / (totals[n : n + 1, :] + extra[128 + n : 129 + n, :])
                inverse[pl.ds(2 * i + n, 1), :] = scale
                own_rows = slice(n * HEAD, (n + 1) * HEAD)
                context_t[rows_at((2 * i + n) * HEAD, HEAD), :] = (
                    (sums[own_rows, :] + extra[own_rows, :]) * scale
                ).astype(BF)

        def keep(h, half):
            return pltpu.make_async_copy((kept_a, kept_b)[half], kept_hbm.at[h], keep_sems.at[half])

        right = right_side(0, 0)
        peak = None
        for t in range(blocks):
            peak = score_tile(0, t, right, scores_a, peak)
        set_peak(0, peak)

        @pl.loop(0, HEADS // 2 - 1)
        def _(i):
            h = i * 2

            @pl.when(i > 0)
            def _():
                keep(h - 2, 0).wait()
            head_step(h, 0, scores_b, scores_a, kept_a, True)
            keep(h, 0).start()

            @pl.when(i > 0)
            def _():
                keep(h - 1, 1).wait()
            head_step(h + 1, 1, scores_a, scores_b, kept_b, True)
            keep(h + 1, 1).start()
            finish_pair(i)
            for n, event in HOPS_IN_LOOP:
                @pl.when(i == n)
                def _():
                    weights.hops((event,))

        h = HEADS - 2
        keep(h - 2, 0).wait()
        head_step(h, 0, scores_b, scores_a, kept_a, True)
        keep(h, 0).start()
        keep(h - 1, 1).wait()
        head_step(h + 1, 1, scores_a, scores_b, kept_b, False)
        keep(h + 1, 1).start()
        finish_pair(HEADS // 2 - 1)
        keep(h, 0).wait()
        keep(h + 1, 1).wait()

    pl.run_scoped(attention, square, square, pltpu.VMEM((SLOT, 128), BF))
    weights.hops(HOPS_AT["attended"])


    def feed_forward(unit, inverse_one, low, active, slope):
        gain_1, shift_1, gain_2, shift_2 = [
            ref[...].astype(F32)[None, :] for ref in (gain_one, shift_one, gain_two, shift_two)]
        everything = slice(0, SLOT)

        def shard_at(j):
            return weights.shard(j // 2, (weights.core + j) % 2)

        def mix(r):
            rs = block(r)
            summed[rs, :] = rows_in[rs, :].astype(F32) + dg(context_t[:, rs], w_output[...], 0, 0)

        def norm_one(r):
            rs = block(r)
            u, inv = norm_parts(summed[rs, :])
            unit[rs, :] = u
            inverse_one[rs, :] = inv
            normed = u * gain_1 + shift_1
            summed[rs, :] = normed
            low[rs, :] = normed.astype(BF)

        def first(j, rs, cols):
            s = shard_at(j)
            pre = jnp.dot(low[rs, :], w_in[s, :, cols], preferred_element_type=F32) + bias[s, 0:1, cols]
            act, slo = gelu_parts(pre)
            active[j % 2, rs, cols] = act
            slope[j, rs, cols] = slo

        def second(j, rs, cols):
            summed[rs, cols] += jnp.dot(active[j % 2, rs, :], w_out[shard_at(j), :, cols], preferred_element_type=F32)

        def norm_two(r):
            rs = block(r)
            u, inv = norm_parts(summed[rs, :])
            upper = norm_back(rows_in[rs, :].astype(F32) * gain_2, u, inv)
            rows_in[rs, :] = (u * gain_2 + shift_2).astype(BF)
            summed[rs, :] = upper
            low[rs, :] = upper.astype(BF)

        def third(j, rs, cols):
            grad = dg(low[rs, :], w_out[shard_at(j), cols, :], 1, 1)
            active[j % 2, rs, cols] = (grad * slope[j, rs, cols].astype(F32)).astype(BF)

        def fourth(j, rs, cols):
            summed[rs, cols] += dg(active[j % 2, rs, :], w_in[shard_at(j), cols, :], 1, 1)

        def norm_one_back(r):
            rs = block(r)
            grad = norm_back(summed[rs, :] * gain_1, unit[rs, :], inverse_one[rs, :])
            summed[rs, :] = grad
            low[rs, :] = grad.astype(BF)

        def parts(function, j, size):
            return [functools.partial(function, j, everything, slice(c, c + TILE)) for c in range(0, size, TILE)]

        def hops(j):
            return [functools.partial(weights.hops, HOPS_AT.get((j, n), ())) for n in range(width // TILE)]

        load_output.wait()
        own[0].wait()
        staged_run([mix, norm_one, lambda r: first(0, block(r), slice(0, hidden))], blocks,
                   lambda step: weights.hops(HOPS_AT.get(("mix", step), ())))
        load_grads.start()
        for d in range(1, shards):
            bias_arrival(d).wait_recv()
        own[1].wait()
        for j in range(1, shards):
            weights.ready(0, j)
            weights.ready(1, j - 1)
            interleave(parts(first, j, hidden), parts(second, j - 1, width), hops(j))
        last = shards - 1
        weights.ready(1, last)
        load_grads.wait()

        whole = slice(0, width)
        staged_run([lambda r: second(last, block(r), whole), norm_two,
                    lambda r: third(0, block(r), slice(0, hidden))], blocks)
        store_output.start()

        @pl.loop(1, shards)
        def _(j):
            interleave(parts(third, j, hidden), parts(fourth, j - 1, width))

        staged_run([lambda r: fourth(last, block(r), whole), norm_one_back], blocks)

        @pl.loop(0, width // TILE)
        def _(g):
            grad = dg(w_output[rows_at(g * TILE, TILE), :], low[...], 1, 1)
            row = lax.broadcasted_iota(jnp.int32, (16, SLOT), 0)
            for i in range(TILE // HEAD):
                h = g * (TILE // HEAD) + i
                rows_h = rows_at(h * HEAD, HEAD)
                scaled = grad[i * HEAD : (i + 1) * HEAD] * inverse[pl.ds(h, 1), :]
                middle = -jnp.sum(scaled * context_t[rows_h, :].astype(F32), axis=0, keepdims=True)
                context_t[rows_h, :] = scaled.astype(BF)
                high = middle.astype(BF).astype(F32)
                both = jnp.where(row == 0, high, jnp.where(row == 1, middle - high, 0.0))
                centre[rows_at(h * 16, 16), :] = both.astype(BF)

    pl.run_scoped(feed_forward, tall, pltpu.VMEM((SLOT, 1), F32), square,
                  pltpu.VMEM((2, SLOT, hidden), BF), pltpu.VMEM((shards, SLOT, hidden), BF))
    weights.finish()
    for d in range(1, shards):
        bias_copy(d).wait_send()


    grad_t = context_t

    def group_copy(d):
        return remote(pieces.at[group_peer(d)], from_group.at[mp], group_sems, d, (dp, group_peer(d)))

    def group_arrival(d):
        place = from_group.at[group_sender(d)]
        return remote(place, place, group_sems, d, (dp, group_peer(d)))

    def rows_copy(d):
        return remote(from_rows.at[dp], from_rows.at[dp], rows_sems, d, ((dp + d) % dp_size, mp))

    def rows_arrival(d):
        place = from_rows.at[(dp - d + dp_size) % dp_size]
        return remote(place, place, rows_sems, d, ((dp + d) % dp_size, mp))

    def attend_back(query_back, key_back, value_back, query_prefix, staged, w_query, w_key, w_value):
        loads = [load(w_query_hbm, w_query, 5), load(w_key_hbm, w_key, 6), load(w_value_hbm, w_value, 7)]

        def copy_in(h, half):
            return pltpu.make_async_copy(kept_hbm.at[h], staged.at[half], keep_sems.at[half])

        copy_in(0, 0).start()
        for copy in loads:
            copy.start()

        @pl.loop(0, HEADS // GROUP)
        def _(g):
            cols = rows_at(g * 256, 256)
            grads = grad_t[cols, :]
            back = jnp.dot(block_diagonal(prefix_value[:, cols]), grads, preferred_element_type=F32)
            parts = []
            for i in range(GROUP):
                h = g * GROUP + i
                middle = jnp.sum(centre[rows_at(h * 16, 16), :].astype(F32), axis=0, keepdims=True)
                kept = kept_prefix[rows_at(h * HEAD, HEAD), :].astype(F32)
                parts.append((kept * (back[i * HEAD : (i + 1) * HEAD] + middle)).astype(BF))
            back = jnp.concatenate(parts, axis=0)
            prefix_grads[:PREFIX, cols] = diagonal_rows(dg(back, query_t[cols, :], 1, 1)) * ln2
            prefix_grads[PREFIX:, cols] = diagonal_rows(dg(kept_prefix[cols, :], grads, 1, 1))
            query_prefix[cols, :] = dg(block_diagonal(prefix_key[:, cols]), back, 0, 0)

        for s in range(shards):
            pieces[s] = prefix_grads[:, s * share : (s + 1) * share]
        for d in range(1, shards):
            group_copy(d).start()

        lane = lax.broadcasted_iota(jnp.int32, (TILE, 128), 1)
        pick = jnp.where(lane < 2, 1.0, 0.0).astype(BF)

        def head_step(h, half):
            rows_h = rows_at(h * HEAD, HEAD)
            pair = rows_at((h // 2) * 128, 128)
            grads = grad_t[rows_h, :]
            zero = jnp.zeros_like(grads)
            last = jnp.concatenate([centre[rows_at(h * 16, 16), :], jnp.zeros((112, SLOT), BF)], axis=0)
            right = jnp.concatenate([grads, zero, last] if half == 0 else [zero, grads, last], axis=0)
            queries = query_t[rows_h, :]
            keys = key_t[rows_h, :]
            total = query_prefix[rows_h, :]
            for t in range(blocks):
                rows = block(t)
                left = jnp.concatenate([value[rows, pair], pick], axis=1)
                back = jnp.dot(left, right, preferred_element_type=F32)
                w = staged[half, rows, :]
                back = (back * w.astype(F32)).astype(BF)
                value_back[rows_h, rows] = dg(grads, w, 1, 1).astype(BF)
                key_back[rows_h, rows] = (dg(queries, back, 1, 1) * ln2).astype(BF)
                total += jnp.dot(keys[:, rows], back, preferred_element_type=F32)
            query_back[rows_h, :] = (total * (1.0 / math.sqrt(HEAD))).astype(BF)

        @pl.loop(0, HEADS // 2)
        def _(i):
            h = i * 2
            copy_in(h, 0).wait()
            copy_in(h + 1, 1).start()
            head_step(h, 0)
            copy_in(h + 1, 1).wait()

            @pl.when(i < HEADS // 2 - 1)
            def _():
                copy_in(h + 2, 0).start()
            head_step(h + 1, 1)

            @pl.when(i == 1)
            def _():
                own_piece = pieces[mp]
                for d in range(1, shards):
                    group_arrival(d).wait_recv()
                    own_piece += from_group[group_sender(d)]
                from_rows[dp] = own_piece
                for d in range(1, dp_size):
                    rows_copy(d).start()

        store_output.wait()
        for copy in loads:
            copy.wait()
        result = rows_in

        def store(r):
            rs = rows_at(r * TILE, TILE)
            return pltpu.make_async_copy(result.at[rs, :], input_grad_hbm.at[rs, :], out_sems.at[r])

        @pl.loop(0, blocks)
        def _(r):
            rs = rows_at(r * TILE, TILE)
            grad = summed[rs, :]
            grad += dg(query_back[:, rs], w_query[...], 0, 1)
            grad += dg(key_back[:, rs], w_key[...], 0, 1)
            grad += dg(value_back[:, rs], w_value[...], 0, 1)
            result[rs, :] = grad.astype(BF)
            store(r).start()

        for d in range(1, dp_size):
            rows_arrival(d).wait_recv()
        total = from_rows[0]
        for n in range(1, dp_size):
            total += from_rows[n]
        key_share[...] = total[:PREFIX]
        value_share[...] = total[PREFIX:]
        for d in range(1, shards):
            group_copy(d).wait_send()
        for d in range(1, dp_size):
            rows_copy(d).wait_send()
        for r in range(blocks):
            store(r).wait()

    pl.run_scoped(attend_back, square, square, square, tall, pltpu.VMEM((2, SLOT, SLOT), BF),
                  *[pltpu.VMEM((width, width), BF)] * 3)


def local(dp_size, shards, tokens, lengths, key_mask, w_query, w_key, w_value, w_output, norm1_gain, norm1_shift,
          w_in, b_in, w_out, norm2_gain, norm2_shift, prefix_key, prefix_value, out_grad):
    rows, width = tokens.shape
    hidden = w_in.shape[1]
    share = width // shards
    chips = shards // 2
    shape = jax.ShapeDtypeStruct
    square = pltpu.VMEM((SLOT, width), BF)
    dma = pltpu.SemaphoreType.DMA
    output, input_grad, key_grad, value_grad, _ = pl.pallas_call(
        functools.partial(layer_kernel, dp_size, shards),
        out_shape=[shape((rows, width), BF), shape((rows, width), BF), shape((PREFIX, share), F32),
                   shape((PREFIX, share), F32), shape((HEADS, SLOT, SLOT), BF)],
        in_specs=[SMEM] + [VMEM] * 8 + [HBM] * 8,
        out_specs=[HBM, HBM, VMEM, VMEM, HBM],
        scratch_shapes=[
            pltpu.VMEM((shards, width, hidden), BF),
            pltpu.VMEM((shards, hidden, width), BF),
            pltpu.VMEM((shards, 8, hidden), F32),
            pltpu.VMEM((shards, 2 * PREFIX, share), F32),
            pltpu.VMEM((shards, 2 * PREFIX, share), F32),
            pltpu.VMEM((dp_size, 2 * PREFIX, share), F32),
            pltpu.VMEM((SLOT, width), F32),
            square, square, square, square, square, square, square,
            pltpu.VMEM((HEADS, SLOT), F32),
            pltpu.VMEM((HEADS * 16, SLOT), BF),
            pltpu.VMEM((8, SLOT), F32),
            pltpu.VMEM((2 * PREFIX, width), F32),
            dma((2, 8, 4 if chips <= 2 else 2, max(chips, 2))),
            dma((2, 2)),
            dma((2, shards)),
            dma((2, shards)),
            dma((2, dp_size)),
            dma((3, SLOT // TILE)),
            dma((8,)),
            dma((2,)),
            dma((SLOT // TILE + 1,)),
        ],
        compiler_params=pltpu.CompilerParams(
            vmem_limit_bytes=63 * 2**20, collective_id=0, has_side_effects=True),
        cost_estimate=pl.CostEstimate(flops=70 * 10**9, bytes_accessed=10**8, transcendentals=3 * 10**7),
        name="layer",
    )(lengths, key_mask.reshape(1, SLOT), norm1_gain, norm1_shift, norm2_gain, norm2_shift, b_in, prefix_key, prefix_value,
      tokens, w_query, w_key, w_value, w_output, w_in, w_out, out_grad)
    return output, input_grad, key_grad, value_grad


def solution(mesh):
    in_specs = (
        P(("dp", "mp"), None), P(("dp", "mp")), P(("dp", "mp")), P(), P(), P(), P(), P(), P(),
        P(None, "mp"), P("mp"), P("mp", None), P(), P(), P(), P(), P(("dp", "mp"), None),
    )
    out_specs = (P(("dp", "mp"), None), P(("dp", "mp"), None), P(None, "mp"), P(None, "mp"))
    return jax.shard_map(
        functools.partial(local, mesh.shape["dp"], mesh.shape["mp"]),
        mesh=mesh, in_specs=in_specs, out_specs=out_specs, check_vma=False)
```

```python
import functools
import math

import jax
import jax.numpy as jnp
from jax import lax
from jax.experimental import pallas as pl
from jax.experimental.pallas import tpu as pltpu
from jax.sharding import PartitionSpec as P

HEADS = 16
HEAD = 64
PREFIX = 64
SLOT = 1024
GROUP = 4
TILE = 256

EPSILON = 1e-05
MASKED = -1e30
LOG2E = 1.4426950408889634
BF = jnp.bfloat16
F32 = jnp.float32

VMEM = pl.BlockSpec(memory_space=pltpu.VMEM)
SMEM = pl.BlockSpec(memory_space=pltpu.SMEM)
HBM = pl.BlockSpec(memory_space=pl.ANY)


def dg(left, right, left_dim, right_dim):
    return lax.dot_general(
        left, right, (((left_dim,), (right_dim,)), ((), ())), preferred_element_type=F32
    )


def rows_at(start, size):
    return pl.ds(pl.multiple_of(start, size), size)


def block_diagonal(part):
    stacked = jnp.concatenate([part] * GROUP, axis=0)
    head_of_row = lax.broadcasted_iota(jnp.int32, stacked.shape, 0) // HEAD
    head_of_column = lax.broadcasted_iota(jnp.int32, stacked.shape, 1) // HEAD
    return jnp.where(head_of_row == head_of_column, stacked, jnp.zeros_like(stacked))


def diagonal_rows(blocks):
    head_of_row = lax.broadcasted_iota(jnp.int32, blocks.shape, 0) // HEAD
    head_of_column = lax.broadcasted_iota(jnp.int32, blocks.shape, 1) // HEAD
    kept = jnp.where(head_of_row == head_of_column, blocks, jnp.zeros_like(blocks))
    return kept[:64] + kept[64:128] + kept[128:192] + kept[192:]


def ones_rows(width):
    row = lax.broadcasted_iota(jnp.int32, (16, width), 0)
    return jnp.where(row == 0, 1.0, 0.0).astype(BF)


def mask_block(length, mask_ref, mask_cols):
    place = lax.broadcasted_iota(jnp.int32, (1, SLOT), 1)
    live = (place < length) & (mask_ref[...] > 0)
    bias = jnp.where(live, 0.0, MASKED)
    row = lax.broadcasted_iota(jnp.int32, (128, SLOT), 0)
    mask_cols[...] = jnp.where(row == 0, bias, 0.0).T.astype(BF)


MESH = pl.DeviceIdType.MESH
HOPS_IN_LOOP = ((0, ("y", 0)), (2, ("y", 1)), (4, ("x", 0)), (4, ("z", 0)), (4, ("y", 2)), (6, ("x", 1)), (6, ("z", 1)))
HOPS_AT = {
    "attended": (("y", 3),),
    ("mix", 1): (("x", 2), ("d", 0)),
    ("mix", 2): (("d", 2),),
    (1, 0): (("z", 2), ("d", 1)),
    (1, 1): (("d", 3),),
    (2, 0): (("x", 3), ("z", 3)),
}


class Weights:
    def __init__(self, sources, gathered, sems, core_sems, dp, mp, shards):
        self.sources, self.gathered, self.sems, self.core_sems = sources, gathered, sems, core_sems
        self.dp, self.mp = dp, mp
        self.core, self.chip, self.chips = mp % 2, mp // 2, shards // 2
        self.a, self.b = dp % 2, (dp // 2) % 2
        self.chunks = 2 if self.chips <= 2 else 1
        self.beside_x = (dp + 1 - 2 * self.a, mp)
        self.beside_z = (dp + 2 - 4 * self.b, mp)
        self.other = (dp, mp + 1 - 2 * (mp % 2))
        self.own_quarter = (self.a, self.b)
        self.x_quarter = (1 - self.a, self.b)
        self.z_quarter = (self.a, 1 - self.b)
        self.far_quarter = (1 - self.a, 1 - self.b)

    def rows(self, which, quarter, c):
        size = self.gathered[which].shape[1] // 4
        step = size // self.chunks
        return pl.ds(pl.multiple_of((quarter[0] * 2 + quarter[1]) * size + c * step, 16), step)

    def shard(self, d, core):
        return ((self.chip - d + self.chips) % self.chips) * 2 + core

    def copy(self, source, target, kind, k, d, device):
        return pltpu.make_async_remote_copy(
            src_ref=source, dst_ref=target, send_sem=self.sems.at[0, kind, k, d],
            recv_sem=self.sems.at[1, kind, k, d], device_id=device, device_id_type=MESH)

    def out_copy(self, k, d):
        which, c = k // self.chunks, k % self.chunks
        rows = self.rows(which, self.own_quarter, c)
        target = ((self.chip + d) % self.chips) * 2 + self.core
        return self.copy(self.sources[which].at[rows, :], self.gathered[which].at[self.mp, rows, :], 0, k, d,
                         (self.dp, target))

    def far_copy(self, k, d):
        which, c = k // self.chunks, k % self.chunks
        rows = self.rows(which, self.far_quarter, c)
        target = ((self.chip + d) % self.chips) * 2 + self.core
        return self.copy(self.sources[which].at[rows, :], self.gathered[which].at[self.mp, rows, :], 3, k, d,
                         (self.dp, target))

    def passed(self, kind, k, d, quarter, device, core=None):
        which, c = k // self.chunks, k % self.chunks
        shard = self.shard(d, self.core if core is None else core)
        place = self.gathered[which].at[shard, self.rows(which, quarter, c), :]
        return self.copy(place, place, kind, k, d, device)

    def across(self, k, d):
        if k % self.chunks == 0:
            return self.passed(3, k, d, self.x_quarter, self.beside_z)
        return self.passed(3, k, d, self.z_quarter, self.beside_x)

    def core_copy(self, which):
        return pltpu.make_async_remote_copy(
            src_ref=self.sources[which], dst_ref=self.gathered[which].at[self.mp],
            send_sem=self.core_sems.at[0, which], recv_sem=self.core_sems.at[1, which],
            device_id=self.other, device_id_type=MESH)

    def core_arrival(self, which):
        place = self.gathered[which].at[self.other[1]]
        return pltpu.make_async_remote_copy(
            src_ref=place, dst_ref=place, send_sem=self.core_sems.at[0, which],
            recv_sem=self.core_sems.at[1, which], device_id=self.other, device_id_type=MESH)

    def start(self):
        for k in range(2 * self.chunks):
            for d in range(1, self.chips):
                self.out_copy(k, d).start()
        for k in range(self.chunks, 2 * self.chunks):
            for d in range(1, self.chips):
                self.far_copy(k, d).start()
        for which in range(2):
            self.core_copy(which).start()

    def arrival(self, event, k, d):
        kind, quarter = {"y": (0, self.own_quarter), "x": (1, self.x_quarter), "z": (2, self.z_quarter),
                         "d": (3, self.far_quarter)}[event]
        return self.passed(kind, k, d, quarter, self.other)

    def onward(self, event, k, d):
        if event == "y":
            return [self.passed(1, k, d, self.own_quarter, self.beside_x),
                    self.passed(2, k, d, self.own_quarter, self.beside_z),
                    self.passed(4, k, d, self.own_quarter, self.other)]
        if event == "d":
            return [self.passed(7, k, d, self.far_quarter, self.other)]
        copies = [self.passed(5, k, d, self.x_quarter, self.other) if event == "x"
                  else self.passed(6, k, d, self.z_quarter, self.other)]
        if k < self.chunks and (k == 0) == (event == "x"):
            copies.append(self.across(k, d))
        return copies

    def hops(self, events):
        for event, k in events:
            if k < 2 * self.chunks:
                for d in range(1, self.chips):
                    self.arrival(event, k, d).wait_recv()
                    for copy in self.onward(event, k, d):
                        copy.start()

    def ready(self, which, j):
        d = j // 2
        if j == 1:
            self.core_arrival(which).wait_recv()
        elif j % 2 == 1:
            for c in range(self.chunks):
                k = which * self.chunks + c
                for kind, quarter in ((4, self.own_quarter), (5, self.x_quarter), (6, self.z_quarter),
                                      (7, self.far_quarter)):
                    self.passed(kind, k, d, quarter, self.other, 1 - self.core).wait_recv()

    def finish(self):
        for k in range(2 * self.chunks):
            for d in range(1, self.chips):
                self.out_copy(k, d).wait_send()
                if k >= self.chunks:
                    self.far_copy(k, d).wait_send()
                for event in "yxzd":
                    for copy in self.onward(event, k, d):
                        copy.wait_send()
        for which in range(2):
            self.core_copy(which).wait_send()


def staged_run(stages, count, after=None):
    for step in range(count + len(stages) - 1):
        for s, stage in enumerate(stages):
            if 0 <= step - s < count:
                stage(step - s)
        if after is not None:
            after(step)


def interleave(*lists):
    for k in range(max(len(parts) for parts in lists)):
        for parts in lists:
            if k < len(parts):
                parts[k]()


def norm_parts(rows):
    centered = rows - jnp.mean(rows, axis=-1, keepdims=True)
    spread = jnp.mean(centered * centered, axis=-1, keepdims=True)
    inverse = lax.rsqrt(spread + EPSILON)
    return centered * inverse, inverse


def norm_back(scaled, unit, inverse):
    first = jnp.mean(scaled, axis=-1, keepdims=True)
    second = jnp.mean(scaled * unit, axis=-1, keepdims=True)
    return inverse * (scaled - first - unit * second)


def gelu_parts(v):
    u = v * (1.0 / math.sqrt(2.0))
    normal = 0.5 * lax.erf(u) + 0.5
    bell = jnp.exp2((u * u) * (-LOG2E))
    return (v * normal).astype(BF), (normal + (u * bell) * (1.0 / math.sqrt(math.pi))).astype(BF)


def layer_kernel(dp_size, shards, length, mask_ref, gain_one, shift_one, gain_two, shift_two, b_in, prefix_key,
                 prefix_value, tokens_hbm, w_query_hbm, w_key_hbm, w_value_hbm, w_output_hbm, w_in_hbm, w_out_hbm,
                 out_grad_hbm, output_hbm, lower_hbm, query_back_hbm, key_back_hbm, value_back_hbm, key_share, value_share, kept_hbm,
                 w_in, w_out, bias, pieces, from_group, from_rows, summed, rows_in, query_t, key_t, value, kept_prefix,
                 context_t, w_output, inverse, centre, peaks, prefix_grads,
                 weight_sems, core_sems, bias_sems, group_sems, rows_sems, part_sems, local_sems, keep_sems, out_sems, back_sems):
    dp, mp = lax.axis_index("dp"), lax.axis_index("mp")
    width = rows_in.shape[1]
    hidden = w_in.shape[2]
    share = width // shards
    blocks = SLOT // TILE
    ln2 = 1.0 / LOG2E
    square = pltpu.VMEM((SLOT, width), BF)
    tall = pltpu.VMEM((SLOT, width), F32)

    barrier = pltpu.get_barrier_semaphore()
    for d in range(1, shards):
        pl.semaphore_signal(barrier, inc=1, device_id=(dp, (mp + d) % shards), device_id_type=MESH)
    for d in range(1, dp_size):
        pl.semaphore_signal(barrier, inc=1, device_id=((dp + d) % dp_size, mp), device_id_type=MESH)

    weights = Weights((w_in_hbm, w_out_hbm), (w_in, w_out), weight_sems, core_sems, dp, mp, shards)

    def remote(source, target, sems, n, device):
        return pltpu.make_async_remote_copy(
            src_ref=source, dst_ref=target, send_sem=sems.at[0, n], recv_sem=sems.at[1, n],
            device_id=device, device_id_type=MESH)

    def load(source, target, n):
        return pltpu.make_async_copy(source, target, local_sems.at[n])

    def group_peer(d):
        return (mp + d) % shards

    def group_sender(d):
        return (mp - d + shards) % shards

    def bias_copy(d):
        return remote(bias.at[mp], bias.at[mp], bias_sems, d, (dp, group_peer(d)))

    def bias_arrival(d):
        place = bias.at[group_sender(d)]
        return remote(place, place, bias_sems, d, (dp, group_peer(d)))

    load(tokens_hbm, rows_in, 0).start()
    own = [load(w_in_hbm, w_in.at[mp], 1), load(w_out_hbm, w_out.at[mp], 2)]
    load_output = load(w_output_hbm, w_output, 3)
    load_grads = load(out_grad_hbm, rows_in, 4)
    store_output = pltpu.make_async_copy(rows_in, output_hbm, out_sems.at[0])
    store_lower = pltpu.make_async_copy(summed, lower_hbm, out_sems.at[1])

    def block(r):
        return slice(r * TILE, (r + 1) * TILE)


    def attention(key, value_t, mask_cols):
        def project(w_query, w_key, w_value):
            def part(n, j):
                cols = rows_at(j * TILE, TILE)
                source = (w_query_hbm, w_key_hbm, w_value_hbm)[n]
                return pltpu.make_async_copy(
                    source.at[:, cols], (w_query, w_key, w_value)[n].at[:, cols], part_sems.at[n, j])

            for j in range(blocks):
                for n in range(3):
                    part(n, j).start()
            for copy in own:
                copy.start()
            load_output.start()
            bias[mp] = jnp.broadcast_to(b_in[...].astype(F32)[None, :], (8, hidden))
            mask_block(length[0], mask_ref, mask_cols)
            load(tokens_hbm, rows_in, 0).wait()

            def columns(j):
                cols = rows_at(j * TILE, TILE)
                part(0, j).wait()
                out = jnp.dot(rows_in[...], w_query[:, cols], preferred_element_type=F32)
                query_t[cols, :] = (out * (LOG2E / math.sqrt(HEAD))).astype(BF).T
                part(1, j).wait()
                out = jnp.dot(rows_in[...], w_key[:, cols], preferred_element_type=F32).astype(BF)
                key[:, cols] = out
                key_t[cols, :] = out.T
                part(2, j).wait()
                out = jnp.dot(rows_in[...], w_value[:, cols], preferred_element_type=F32).astype(BF)
                value[:, cols] = out
                value_t[cols, :] = out.T

            pl.loop(0, 1)(columns)
            pl.semaphore_wait(barrier, shards - 1 + dp_size - 1)
            weights.start()
            for d in range(1, shards):
                bias_copy(d).start()
            pl.loop(1, blocks)(columns)

        pl.run_scoped(project, *[pltpu.VMEM((width, width), BF)] * 3)
        long = pltpu.VMEM((SLOT + PREFIX, SLOT), F32)
        kept = pltpu.VMEM((SLOT, SLOT), BF)
        pl.run_scoped(functools.partial(attend, key, value_t, mask_cols), long, long, kept, kept,
                      pltpu.VMEM((2 * HEAD, SLOT), F32), pltpu.VMEM((8, SLOT), F32))

    def attend(key, value_t, mask_cols, scores_a, scores_b, kept_a, kept_b, sums, totals):
        prefix_rows = slice(SLOT, SLOT + PREFIX)

        def right_side(h, half):
            q = query_t[rows_at(h * HEAD, HEAD), :]
            zero = jnp.zeros_like(q)
            last = jnp.concatenate([ones_rows(SLOT), jnp.zeros((112, SLOT), BF)], axis=0)
            return jnp.concatenate([q, zero, last] if half == 0 else [zero, q, last], axis=0)

        def folded(s):
            return jnp.max(s.reshape(s.shape[0] // 8, 8, SLOT), axis=0)

        def score_tile(h, t, right, scores, peak):
            rows = block(t)
            pair = rows_at((h // 2) * 128, 128)
            left = jnp.concatenate([key[rows, pair], mask_cols[rows, :]], axis=1)
            s = jnp.dot(left, right, preferred_element_type=F32)
            scores[rows, :] = s
            peak = folded(s) if peak is None else jnp.maximum(peak, folded(s))
            if t == blocks - 1:
                left = jnp.concatenate([prefix_key[:, pair], jnp.zeros((PREFIX, 128), BF)], axis=1)
                s = jnp.dot(left, right, preferred_element_type=F32)
                scores[prefix_rows, :] = s
                peak = jnp.maximum(peak, folded(s))
            return peak

        def set_peak(half, peak):
            peaks[half : half + 1, :] = jnp.max(peak, axis=0, keepdims=True)

        def head_step(h, half, scores_new, scores_old, kept, more):
            if more:
                right = right_side(h + 1, 1 - half)
            top = peaks[half : half + 1, :]
            rows_h = rows_at(h * HEAD, HEAD)
            left = jnp.concatenate([value_t[rows_h, :], ones_rows(SLOT)], axis=0)
            total = jnp.zeros((80, SLOT), F32)
            peak = None
            for t in range(blocks):
                rows = block(t)
                if more:
                    peak = score_tile(h + 1, t, right, scores_new, peak)
                p = jnp.exp2(scores_old[rows, :] - top).astype(BF)
                kept[rows, :] = p
                total += jnp.dot(left[:, rows], p, preferred_element_type=F32)
            kept_prefix[rows_h, :] = jnp.exp2(scores_old[prefix_rows, :] - top).astype(BF)
            if more:
                set_peak(1 - half, peak)
            sums[half * HEAD : (half + 1) * HEAD, :] = total[:HEAD]
            totals[half : half + 1, :] = total[HEAD : HEAD + 1]

        def finish_pair(i):
            pair = rows_at(i * 128, 128)
            row = lax.broadcasted_iota(jnp.int32, (128, 256), 0) // HEAD
            column = lax.broadcasted_iota(jnp.int32, (128, 256), 1)
            part = prefix_value[:, pair]
            both = jnp.concatenate([part, part], axis=0)
            both = jnp.concatenate([both, jnp.ones((128, 128), BF)], axis=1)
            wanted = jnp.where(column < 128, column // HEAD, column - 128)
            left = jnp.where(row == wanted, both, jnp.zeros_like(both))
            extra = dg(left, kept_prefix[pair, :], 0, 0)
            for n in range(2):
                scale = 1.0 / (totals[n : n + 1, :] + extra[128 + n : 129 + n, :])
                inverse[pl.ds(2 * i + n, 1), :] = scale
                own_rows = slice(n * HEAD, (n + 1) * HEAD)
                context_t[rows_at((2 * i + n) * HEAD, HEAD), :] = (
                    (sums[own_rows, :] + extra[own_rows, :]) * scale
                ).astype(BF)

        def keep(h, half):
            return pltpu.make_async_copy((kept_a, kept_b)[half], kept_hbm.at[h], keep_sems.at[half])

        right = right_side(0, 0)
        peak = None
        for t in range(blocks):
            peak = score_tile(0, t, right, scores_a, peak)
        set_peak(0, peak)

        @pl.loop(0, HEADS // 2 - 1)
        def _(i):
            h = i * 2

            @pl.when(i > 0)
            def _():
                keep(h - 2, 0).wait()
            head_step(h, 0, scores_b, scores_a, kept_a, True)
            keep(h, 0).start()

            @pl.when(i > 0)
            def _():
                keep(h - 1, 1).wait()
            head_step(h + 1, 1, scores_a, scores_b, kept_b, True)
            keep(h + 1, 1).start()
            finish_pair(i)
            for n, event in HOPS_IN_LOOP:
                @pl.when(i == n)
                def _():
                    weights.hops((event,))

        h = HEADS - 2
        keep(h - 2, 0).wait()
        head_step(h, 0, scores_b, scores_a, kept_a, True)
        keep(h, 0).start()
        keep(h - 1, 1).wait()
        head_step(h + 1, 1, scores_a, scores_b, kept_b, False)
        keep(h + 1, 1).start()
        finish_pair(HEADS // 2 - 1)
        keep(h, 0).wait()
        keep(h + 1, 1).wait()

    pl.run_scoped(attention, square, square, pltpu.VMEM((SLOT, 128), BF))
    weights.hops(HOPS_AT["attended"])


    def feed_forward(unit, inverse_one, low, active_even, active_odd, slope):
        active = (active_even, active_odd)
        gain_1, shift_1, gain_2, shift_2 = [
            ref[...].astype(F32)[None, :] for ref in (gain_one, shift_one, gain_two, shift_two)]
        everything = slice(0, SLOT)

        def shard_at(j):
            return weights.shard(j // 2, (weights.core + j) % 2)

        def mix(r):
            rs = block(r)
            summed[rs, :] = rows_in[rs, :].astype(F32) + dg(context_t[:, rs], w_output[...], 0, 0)

        def norm_one(r):
            rs = block(r)
            u, inv = norm_parts(summed[rs, :])
            unit[rs, :] = u
            inverse_one[rs, :] = inv
            normed = u * gain_1 + shift_1
            summed[rs, :] = normed
            low[rs, :] = normed.astype(BF)

        def first(j, rs, cols):
            s = shard_at(j)
            pre = jnp.dot(low[rs, :], w_in[s, :, cols], preferred_element_type=F32) + bias[s, 0:1, cols]
            act, slo = gelu_parts(pre)
            active[j % 2][rs, cols] = act
            slope[j, rs, cols] = slo

        def second(j, rs, cols):
            summed[rs, cols] += jnp.dot(active[j % 2][rs, :], w_out[shard_at(j), :, cols], preferred_element_type=F32)

        def norm_two(r):
            rs = block(r)
            u, inv = norm_parts(summed[rs, :])
            upper = norm_back(rows_in[rs, :].astype(F32) * gain_2, u, inv)
            rows_in[rs, :] = (u * gain_2 + shift_2).astype(BF)
            summed[rs, :] = upper
            low[rs, :] = upper.astype(BF)

        def third(j, rs, cols):
            grad = dg(low[rs, :], w_out[shard_at(j), cols, :], 1, 1)
            active[j % 2][rs, cols] = (grad * slope[j, rs, cols].astype(F32)).astype(BF)

        def fourth(j, rs, cols):
            summed[rs, cols] += dg(active[j % 2][rs, :], w_in[shard_at(j), cols, :], 1, 1)

        def norm_one_back(r):
            rs = block(r)
            grad = norm_back(summed[rs, :] * gain_1, unit[rs, :], inverse_one[rs, :])
            summed[rs, :] = grad
            low[rs, :] = grad.astype(BF)

        def parts(function, j, size):
            return [functools.partial(function, j, everything, slice(c, c + TILE)) for c in range(0, size, TILE)]

        def hops(j):
            return [functools.partial(weights.hops, HOPS_AT.get((j, n), ())) for n in range(width // TILE)]

        load_output.wait()
        own[0].wait()
        staged_run([mix, norm_one, lambda r: first(0, block(r), slice(0, hidden))], blocks,
                   lambda step: weights.hops(HOPS_AT.get(("mix", step), ())))
        load_grads.start()
        for d in range(1, shards):
            bias_arrival(d).wait_recv()
        own[1].wait()
        for j in range(1, shards):
            weights.ready(0, j)
            weights.ready(1, j - 1)
            interleave(parts(first, j, hidden), parts(second, j - 1, width), hops(j))
        last = shards - 1
        weights.ready(1, last)
        load_grads.wait()

        whole = slice(0, width)
        staged_run([lambda r: second(last, block(r), whole), norm_two,
                    lambda r: third(0, block(r), slice(0, hidden))], blocks)
        store_output.start()
        for j in range(1, shards):
            interleave(parts(third, j, hidden), parts(fourth, j - 1, width))
        staged_run([lambda r: fourth(last, block(r), whole), norm_one_back], blocks)

        @pl.loop(0, width // TILE)
        def _(g):
            grad = dg(w_output[rows_at(g * TILE, TILE), :], low[...], 1, 1)
            row = lax.broadcasted_iota(jnp.int32, (16, SLOT), 0)
            for i in range(TILE // HEAD):
                h = g * (TILE // HEAD) + i
                rows_h = rows_at(h * HEAD, HEAD)
                scaled = grad[i * HEAD : (i + 1) * HEAD] * inverse[pl.ds(h, 1), :]
                middle = -jnp.sum(scaled * context_t[rows_h, :].astype(F32), axis=0, keepdims=True)
                context_t[rows_h, :] = scaled.astype(BF)
                high = middle.astype(BF).astype(F32)
                both = jnp.where(row == 0, high, jnp.where(row == 1, middle - high, 0.0))
                centre[rows_at(h * 16, 16), :] = both.astype(BF)

    pl.run_scoped(feed_forward, tall, pltpu.VMEM((SLOT, 1), F32), square,
                  pltpu.VMEM((SLOT, hidden), BF), pltpu.VMEM((SLOT, hidden), BF),
                  pltpu.VMEM((shards, SLOT, hidden), BF))
    weights.finish()
    for d in range(1, shards):
        bias_copy(d).wait_send()


    grad_t = context_t

    def group_copy(d):
        return remote(pieces.at[group_peer(d)], from_group.at[mp], group_sems, d, (dp, group_peer(d)))

    def group_arrival(d):
        place = from_group.at[group_sender(d)]
        return remote(place, place, group_sems, d, (dp, group_peer(d)))

    def rows_copy(d):
        return remote(from_rows.at[dp], from_rows.at[dp], rows_sems, d, ((dp + d) % dp_size, mp))

    def rows_arrival(d):
        place = from_rows.at[(dp - d + dp_size) % dp_size]
        return remote(place, place, rows_sems, d, ((dp + d) % dp_size, mp))

    def attend_back(query_back, key_back, value_back, query_prefix, staged):
        store_lower.start()

        def copy_in(h, half):
            return pltpu.make_async_copy(kept_hbm.at[h], staged.at[half], keep_sems.at[half])

        def stores(i):
            rows = rows_at(i * 128, 128)
            return [pltpu.make_async_copy(source.at[rows, :], target.at[rows, :], back_sems.at[n, i])
                    for n, (source, target) in enumerate(
                        ((query_back, query_back_hbm), (key_back, key_back_hbm), (value_back, value_back_hbm)))]

        copy_in(0, 0).start()

        @pl.loop(0, HEADS // GROUP)
        def _(g):
            cols = rows_at(g * 256, 256)
            grads = grad_t[cols, :]
            back = jnp.dot(block_diagonal(prefix_value[:, cols]), grads, preferred_element_type=F32)
            parts = []
            for i in range(GROUP):
                h = g * GROUP + i
                middle = jnp.sum(centre[rows_at(h * 16, 16), :].astype(F32), axis=0, keepdims=True)
                kept = kept_prefix[rows_at(h * HEAD, HEAD), :].astype(F32)
                parts.append((kept * (back[i * HEAD : (i + 1) * HEAD] + middle)).astype(BF))
            back = jnp.concatenate(parts, axis=0)
            prefix_grads[:PREFIX, cols] = diagonal_rows(dg(back, query_t[cols, :], 1, 1)) * ln2
            prefix_grads[PREFIX:, cols] = diagonal_rows(dg(kept_prefix[cols, :], grads, 1, 1))
            query_prefix[cols, :] = dg(block_diagonal(prefix_key[:, cols]), back, 0, 0)

        for s in range(shards):
            pieces[s] = prefix_grads[:, s * share : (s + 1) * share]
        for d in range(1, shards):
            group_copy(d).start()

        lane = lax.broadcasted_iota(jnp.int32, (TILE, 128), 1)
        pick = jnp.where(lane < 2, 1.0, 0.0).astype(BF)

        def head_step(h, half):
            rows_h = rows_at(h * HEAD, HEAD)
            pair = rows_at((h // 2) * 128, 128)
            grads = grad_t[rows_h, :]
            zero = jnp.zeros_like(grads)
            last = jnp.concatenate([centre[rows_at(h * 16, 16), :], jnp.zeros((112, SLOT), BF)], axis=0)
            right = jnp.concatenate([grads, zero, last] if half == 0 else [zero, grads, last], axis=0)
            queries = query_t[rows_h, :]
            keys = key_t[rows_h, :]
            total = query_prefix[rows_h, :]
            for t in range(blocks):
                rows = block(t)
                left = jnp.concatenate([value[rows, pair], pick], axis=1)
                back = jnp.dot(left, right, preferred_element_type=F32)
                w = staged[half, rows, :]
                back = (back * w.astype(F32)).astype(BF)
                value_back[rows_h, rows] = dg(grads, w, 1, 1).astype(BF)
                key_back[rows_h, rows] = (dg(queries, back, 1, 1) * ln2).astype(BF)
                total += jnp.dot(keys[:, rows], back, preferred_element_type=F32)
            query_back[rows_h, :] = (total * (1.0 / math.sqrt(HEAD))).astype(BF)

        @pl.loop(0, HEADS // 2)
        def _(i):
            h = i * 2
            copy_in(h, 0).wait()
            copy_in(h + 1, 1).start()
            head_step(h, 0)
            copy_in(h + 1, 1).wait()

            @pl.when(i < HEADS // 2 - 1)
            def _():
                copy_in(h + 2, 0).start()
            head_step(h + 1, 1)
            for copy in stores(i):
                copy.start()

            @pl.when(i == 1)
            def _():
                own_piece = pieces[mp]
                for d in range(1, shards):
                    group_arrival(d).wait_recv()
                    own_piece += from_group[group_sender(d)]
                from_rows[dp] = own_piece
                for d in range(1, dp_size):
                    rows_copy(d).start()

        for d in range(1, dp_size):
            rows_arrival(d).wait_recv()
        total = from_rows[0]
        for n in range(1, dp_size):
            total += from_rows[n]
        key_share[...] = total[:PREFIX]
        value_share[...] = total[PREFIX:]
        for d in range(1, shards):
            group_copy(d).wait_send()
        for d in range(1, dp_size):
            rows_copy(d).wait_send()
        for i in range(HEADS // 2):
            for copy in stores(i):
                copy.wait()
        store_output.wait()
        store_lower.wait()

    pl.run_scoped(attend_back, square, square, square, tall, pltpu.VMEM((2, SLOT, SLOT), BF))


def finish_kernel(output_from, key_from, value_from, lower_hbm, query_back_hbm, key_back_hbm, value_back_hbm,
                  w_query_hbm, w_key_hbm, w_value_hbm, output_hbm, input_grad_hbm, key_hbm, value_hbm,
                  total, result, lower, back, weights, passing, passing_key, passing_value,
                  back_sems, weight_sems, load_sems, store_sems):
    blocks = SLOT // TILE
    sources = ((query_back_hbm, w_query_hbm), (key_back_hbm, w_key_hbm), (value_back_hbm, w_value_hbm))
    loads = [(pltpu.make_async_copy(source, back.at[n], back_sems.at[n]),
              pltpu.make_async_copy(weight, weights.at[n], weight_sems.at[n]))
             for n, (source, weight) in enumerate(sources)]
    passed = ((output_from, passing, output_hbm), (key_from, passing_key, key_hbm),
              (value_from, passing_value, value_hbm))
    fetches = [pltpu.make_async_copy(source, middle, load_sems.at[n])
               for n, (source, middle, _) in enumerate(passed)]
    stores = [pltpu.make_async_copy(middle, target, store_sems.at[blocks + n])
              for n, (_, middle, target) in enumerate(passed)]
    load_lower = pltpu.make_async_copy(lower_hbm, lower, load_sems.at[3])
    for pair in loads:
        for copy in pair:
            copy.start()
    for copy in fetches:
        copy.start()
    load_lower.start()
    for n in range(3):
        for copy in loads[n]:
            copy.wait()
        if n == 2:
            for fetch, store in zip(fetches, stores):
                fetch.wait()
                store.start()
            load_lower.wait()
        for r in range(blocks):
            rs = slice(r * TILE, (r + 1) * TILE)
            grad = dg(back[n, :, rs], weights[n], 0, 1)
            if n == 0:
                total[rs, :] = grad
            elif n == 1:
                total[rs, :] += grad
            else:
                result[rs, :] = (lower[rs, :] + total[rs, :] + grad).astype(BF)
                store = pltpu.make_async_copy(result.at[rs, :], input_grad_hbm.at[rs, :], store_sems.at[r])
                store.start()
                stores.append(store)
    for copy in stores:
        copy.wait()


def local(dp_size, shards, tokens, lengths, key_mask, w_query, w_key, w_value, w_output, norm1_gain, norm1_shift,
          w_in, b_in, w_out, norm2_gain, norm2_shift, prefix_key, prefix_value, out_grad):
    rows, width = tokens.shape
    hidden = w_in.shape[1]
    share = width // shards
    chips = shards // 2
    shape = jax.ShapeDtypeStruct
    square = pltpu.VMEM((SLOT, width), BF)
    dma = pltpu.SemaphoreType.DMA
    output, lower, query_back, key_back, value_back, key_grad, value_grad, _ = pl.pallas_call(
        functools.partial(layer_kernel, dp_size, shards),
        out_shape=[shape((rows, width), BF), shape((rows, width), F32)] + [shape((width, SLOT), BF)] * 3
        + [shape((PREFIX, share), F32)] * 2 + [shape((HEADS, SLOT, SLOT), BF)],
        in_specs=[SMEM] + [VMEM] * 8 + [HBM] * 8,
        out_specs=[HBM] * 5 + [VMEM, VMEM, HBM],
        scratch_shapes=[
            pltpu.VMEM((shards, width, hidden), BF),
            pltpu.VMEM((shards, hidden, width), BF),
            pltpu.VMEM((shards, 8, hidden), F32),
            pltpu.VMEM((shards, 2 * PREFIX, share), F32),
            pltpu.VMEM((shards, 2 * PREFIX, share), F32),
            pltpu.VMEM((dp_size, 2 * PREFIX, share), F32),
            pltpu.VMEM((SLOT, width), F32),
            square, square, square, square, square, square, square,
            pltpu.VMEM((HEADS, SLOT), F32),
            pltpu.VMEM((HEADS * 16, SLOT), BF),
            pltpu.VMEM((8, SLOT), F32),
            pltpu.VMEM((2 * PREFIX, width), F32),
            dma((2, 8, 4 if chips <= 2 else 2, max(chips, 2))),
            dma((2, 2)),
            dma((2, shards)),
            dma((2, shards)),
            dma((2, dp_size)),
            dma((3, SLOT // TILE)),
            dma((8,)),
            dma((2,)),
            dma((2,)),
            dma((3, HEADS // 2)),
        ],
        compiler_params=pltpu.CompilerParams(
            vmem_limit_bytes=63 * 2**20, collective_id=0, has_side_effects=True),
        cost_estimate=pl.CostEstimate(flops=70 * 10**9, bytes_accessed=10**8, transcendentals=3 * 10**7),
        name="layer",
    )(lengths, key_mask.reshape(1, SLOT), norm1_gain, norm1_shift, norm2_gain, norm2_shift, b_in, prefix_key, prefix_value,
      tokens, w_query, w_key, w_value, w_output, w_in, w_out, out_grad)
    return pl.pallas_call(
        finish_kernel,
        out_shape=[shape((rows, width), BF)] * 2 + [shape((PREFIX, share), F32)] * 2,
        in_specs=[HBM] * 10,
        out_specs=[HBM] * 4,
        scratch_shapes=[
            pltpu.VMEM((SLOT, width), F32),
            square,
            pltpu.VMEM((SLOT, width), F32),
            pltpu.VMEM((3, width, SLOT), BF),
            pltpu.VMEM((3, width, width), BF),
            square,
            pltpu.VMEM((PREFIX, share), F32),
            pltpu.VMEM((PREFIX, share), F32),
            dma((3,)),
            dma((3,)),
            dma((4,)),
            dma((SLOT // TILE + 3,)),
        ],
        compiler_params=pltpu.CompilerParams(vmem_limit_bytes=60 * 2**20),
        cost_estimate=pl.CostEstimate(flops=7 * 10**9, bytes_accessed=3 * 10**7, transcendentals=0),
        name="finish",
    )(output, key_grad, value_grad, lower, query_back, key_back, value_back, w_query, w_key, w_value)


def solution(mesh):
    in_specs = (
        P(("dp", "mp"), None), P(("dp", "mp")), P(("dp", "mp")), P(), P(), P(), P(), P(), P(),
        P(None, "mp"), P("mp"), P("mp", None), P(), P(), P(), P(), P(("dp", "mp"), None),
    )
    out_specs = (P(("dp", "mp"), None), P(("dp", "mp"), None), P(None, "mp"), P(None, "mp"))
    return jax.shard_map(
        functools.partial(local, mesh.shape["dp"], mesh.shape["mp"]),
        mesh=mesh, in_specs=in_specs, out_specs=out_specs, check_vma=False)
```

```python
import functools
import math

import jax
import jax.numpy as jnp
from jax import lax
from jax.experimental import pallas as pl
from jax.experimental.pallas import tpu as pltpu
from jax.sharding import PartitionSpec as P

HEADS = 16
HEAD = 64
PREFIX = 64
SLOT = 1024
GROUP = 4
TILE = 256

EPSILON = 1e-05
MASKED = -1e30
LOG2E = 1.4426950408889634
BF = jnp.bfloat16
F32 = jnp.float32

VMEM = pl.BlockSpec(memory_space=pltpu.VMEM)
SMEM = pl.BlockSpec(memory_space=pltpu.SMEM)
HBM = pl.BlockSpec(memory_space=pl.ANY)


def dg(left, right, left_dim, right_dim):
    return lax.dot_general(
        left, right, (((left_dim,), (right_dim,)), ((), ())), preferred_element_type=F32
    )


def rows_at(start, size):
    return pl.ds(pl.multiple_of(start, size), size)


def block_diagonal(part):
    stacked = jnp.concatenate([part] * GROUP, axis=0)
    head_of_row = lax.broadcasted_iota(jnp.int32, stacked.shape, 0) // HEAD
    head_of_column = lax.broadcasted_iota(jnp.int32, stacked.shape, 1) // HEAD
    return jnp.where(head_of_row == head_of_column, stacked, jnp.zeros_like(stacked))


def diagonal_rows(blocks):
    head_of_row = lax.broadcasted_iota(jnp.int32, blocks.shape, 0) // HEAD
    head_of_column = lax.broadcasted_iota(jnp.int32, blocks.shape, 1) // HEAD
    kept = jnp.where(head_of_row == head_of_column, blocks, jnp.zeros_like(blocks))
    return kept[:64] + kept[64:128] + kept[128:192] + kept[192:]


def ones_rows(width):
    row = lax.broadcasted_iota(jnp.int32, (16, width), 0)
    return jnp.where(row == 0, 1.0, 0.0).astype(BF)


def mask_block(length, mask_ref, mask_cols):
    place = lax.broadcasted_iota(jnp.int32, (1, SLOT), 1)
    live = (place < length) & (mask_ref[...] > 0)
    bias = jnp.where(live, 0.0, MASKED)
    row = lax.broadcasted_iota(jnp.int32, (128, SLOT), 0)
    mask_cols[...] = jnp.where(row == 0, bias, 0.0).T.astype(BF)


MESH = pl.DeviceIdType.MESH
HOPS_IN_LOOP = ((0, ("y", 0)), (2, ("y", 1)), (4, ("x", 0)), (4, ("z", 0)), (4, ("y", 2)), (6, ("x", 1)), (6, ("z", 1)))
HOPS_AT = {
    "attended": (("y", 3),),
    ("mix", 1): (("x", 2), ("d", 0)),
    ("mix", 2): (("d", 2),),
    (1, 0): (("z", 2), ("d", 1)),
    (1, 1): (("d", 3),),
    (2, 0): (("x", 3), ("z", 3)),
}


class Weights:
    def __init__(self, sources, gathered, sems, core_sems, dp, mp, shards):
        self.sources, self.gathered, self.sems, self.core_sems = sources, gathered, sems, core_sems
        self.dp, self.mp = dp, mp
        self.core, self.chip, self.chips = mp % 2, mp // 2, shards // 2
        self.a, self.b = dp % 2, (dp // 2) % 2
        self.chunks = 2 if self.chips <= 2 else 1
        self.beside_x = (dp + 1 - 2 * self.a, mp)
        self.beside_z = (dp + 2 - 4 * self.b, mp)
        self.other = (dp, mp + 1 - 2 * (mp % 2))
        self.own_quarter = (self.a, self.b)
        self.x_quarter = (1 - self.a, self.b)
        self.z_quarter = (self.a, 1 - self.b)
        self.far_quarter = (1 - self.a, 1 - self.b)

    def rows(self, which, quarter, c):
        size = self.gathered[which].shape[1] // 4
        step = size // self.chunks
        return pl.ds(pl.multiple_of((quarter[0] * 2 + quarter[1]) * size + c * step, 16), step)

    def shard(self, d, core):
        return ((self.chip - d + self.chips) % self.chips) * 2 + core

    def copy(self, source, target, kind, k, d, device):
        return pltpu.make_async_remote_copy(
            src_ref=source, dst_ref=target, send_sem=self.sems.at[0, kind, k, d],
            recv_sem=self.sems.at[1, kind, k, d], device_id=device, device_id_type=MESH)

    def out_copy(self, k, d):
        which, c = k // self.chunks, k % self.chunks
        rows = self.rows(which, self.own_quarter, c)
        target = ((self.chip + d) % self.chips) * 2 + self.core
        return self.copy(self.sources[which].at[rows, :], self.gathered[which].at[self.mp, rows, :], 0, k, d,
                         (self.dp, target))

    def far_copy(self, k, d):
        which, c = k // self.chunks, k % self.chunks
        rows = self.rows(which, self.far_quarter, c)
        target = ((self.chip + d) % self.chips) * 2 + self.core
        return self.copy(self.sources[which].at[rows, :], self.gathered[which].at[self.mp, rows, :], 3, k, d,
                         (self.dp, target))

    def passed(self, kind, k, d, quarter, device, core=None):
        which, c = k // self.chunks, k % self.chunks
        shard = self.shard(d, self.core if core is None else core)
        place = self.gathered[which].at[shard, self.rows(which, quarter, c), :]
        return self.copy(place, place, kind, k, d, device)

    def across(self, k, d):
        if k % self.chunks == 0:
            return self.passed(3, k, d, self.x_quarter, self.beside_z)
        return self.passed(3, k, d, self.z_quarter, self.beside_x)

    def core_copy(self, which):
        return pltpu.make_async_remote_copy(
            src_ref=self.sources[which], dst_ref=self.gathered[which].at[self.mp],
            send_sem=self.core_sems.at[0, which], recv_sem=self.core_sems.at[1, which],
            device_id=self.other, device_id_type=MESH)

    def core_arrival(self, which):
        place = self.gathered[which].at[self.other[1]]
        return pltpu.make_async_remote_copy(
            src_ref=place, dst_ref=place, send_sem=self.core_sems.at[0, which],
            recv_sem=self.core_sems.at[1, which], device_id=self.other, device_id_type=MESH)

    def start(self):
        for k in range(2 * self.chunks):
            for d in range(1, self.chips):
                self.out_copy(k, d).start()
        for k in range(self.chunks, 2 * self.chunks):
            for d in range(1, self.chips):
                self.far_copy(k, d).start()
        for which in range(2):
            self.core_copy(which).start()

    def arrival(self, event, k, d):
        kind, quarter = {"y": (0, self.own_quarter), "x": (1, self.x_quarter), "z": (2, self.z_quarter),
                         "d": (3, self.far_quarter)}[event]
        return self.passed(kind, k, d, quarter, self.other)

    def onward(self, event, k, d):
        if event == "y":
            return [self.passed(1, k, d, self.own_quarter, self.beside_x),
                    self.passed(2, k, d, self.own_quarter, self.beside_z),
                    self.passed(4, k, d, self.own_quarter, self.other)]
        if event == "d":
            return [self.passed(7, k, d, self.far_quarter, self.other)]
        copies = [self.passed(5, k, d, self.x_quarter, self.other) if event == "x"
                  else self.passed(6, k, d, self.z_quarter, self.other)]
        if k < self.chunks and (k == 0) == (event == "x"):
            copies.append(self.across(k, d))
        return copies

    def hops(self, events):
        for event, k in events:
            if k < 2 * self.chunks:
                for d in range(1, self.chips):
                    self.arrival(event, k, d).wait_recv()
                    for copy in self.onward(event, k, d):
                        copy.start()

    def ready(self, which, j):
        d = j // 2
        if j == 1:
            self.core_arrival(which).wait_recv()
        elif j % 2 == 1:
            for c in range(self.chunks):
                k = which * self.chunks + c
                for kind, quarter in ((4, self.own_quarter), (5, self.x_quarter), (6, self.z_quarter),
                                      (7, self.far_quarter)):
                    self.passed(kind, k, d, quarter, self.other, 1 - self.core).wait_recv()

    def finish(self):
        for k in range(2 * self.chunks):
            for d in range(1, self.chips):
                self.out_copy(k, d).wait_send()
                if k >= self.chunks:
                    self.far_copy(k, d).wait_send()
                for event in "yxzd":
                    for copy in self.onward(event, k, d):
                        copy.wait_send()
        for which in range(2):
            self.core_copy(which).wait_send()


def staged_run(stages, count, after=None):
    for step in range(count + len(stages) - 1):
        for s, stage in enumerate(stages):
            if 0 <= step - s < count:
                stage(step - s)
        if after is not None:
            after(step)


def interleave(*lists):
    for k in range(max(len(parts) for parts in lists)):
        for parts in lists:
            if k < len(parts):
                parts[k]()


def norm_parts(rows):
    centered = rows - jnp.mean(rows, axis=-1, keepdims=True)
    spread = jnp.mean(centered * centered, axis=-1, keepdims=True)
    inverse = lax.rsqrt(spread + EPSILON)
    return centered * inverse, inverse


def norm_back(scaled, unit, inverse):
    first = jnp.mean(scaled, axis=-1, keepdims=True)
    second = jnp.mean(scaled * unit, axis=-1, keepdims=True)
    return inverse * (scaled - first - unit * second)


def gelu_parts(v):
    u = v * (1.0 / math.sqrt(2.0))
    normal = 0.5 * lax.erf(u) + 0.5
    bell = jnp.exp2((u * u) * (-LOG2E))
    return (v * normal).astype(BF), (normal + (u * bell) * (1.0 / math.sqrt(math.pi))).astype(BF)


def layer_kernel(dp_size, shards, length, mask_ref, gain_one, shift_one, gain_two, shift_two, b_in, prefix_key,
                 prefix_value, tokens_hbm, w_query_hbm, w_key_hbm, w_value_hbm, w_output_hbm, w_in_hbm, w_out_hbm,
                 out_grad_hbm, output_hbm, lower_hbm, query_back_hbm, key_back_hbm, value_back_hbm, key_share, value_share, kept_hbm,
                 w_in, w_out, bias, pieces, from_group, from_rows, summed, rows_in, query_t, key_t, value, kept_prefix,
                 context_t, w_output, inverse, centre, peaks, prefix_grads,
                 weight_sems, core_sems, bias_sems, group_sems, rows_sems, part_sems, local_sems, keep_sems, out_sems, back_sems):
    dp, mp = lax.axis_index("dp"), lax.axis_index("mp")
    width = rows_in.shape[1]
    hidden = w_in.shape[2]
    share = width // shards
    blocks = SLOT // TILE
    ln2 = 1.0 / LOG2E
    square = pltpu.VMEM((SLOT, width), BF)
    tall = pltpu.VMEM((SLOT, width), F32)

    barrier = pltpu.get_barrier_semaphore()
    for d in range(1, shards):
        pl.semaphore_signal(barrier, inc=1, device_id=(dp, (mp + d) % shards), device_id_type=MESH)
    for d in range(1, dp_size):
        pl.semaphore_signal(barrier, inc=1, device_id=((dp + d) % dp_size, mp), device_id_type=MESH)

    weights = Weights((w_in_hbm, w_out_hbm), (w_in, w_out), weight_sems, core_sems, dp, mp, shards)

    def remote(source, target, sems, n, device):
        return pltpu.make_async_remote_copy(
            src_ref=source, dst_ref=target, send_sem=sems.at[0, n], recv_sem=sems.at[1, n],
            device_id=device, device_id_type=MESH)

    def load(source, target, n):
        return pltpu.make_async_copy(source, target, local_sems.at[n])

    def group_peer(d):
        return (mp + d) % shards

    def group_sender(d):
        return (mp - d + shards) % shards

    def bias_copy(d):
        return remote(bias.at[mp], bias.at[mp], bias_sems, d, (dp, group_peer(d)))

    def bias_arrival(d):
        place = bias.at[group_sender(d)]
        return remote(place, place, bias_sems, d, (dp, group_peer(d)))

    load(tokens_hbm, rows_in, 0).start()
    own = [load(w_in_hbm, w_in.at[mp], 1), load(w_out_hbm, w_out.at[mp], 2)]
    load_output = load(w_output_hbm, w_output, 3)
    load_grads = load(out_grad_hbm, rows_in, 4)
    store_output = pltpu.make_async_copy(rows_in, output_hbm, out_sems.at[0])
    store_lower = pltpu.make_async_copy(summed, lower_hbm, out_sems.at[1])

    def block(r):
        return slice(r * TILE, (r + 1) * TILE)


    def attention(key, value_t, mask_cols):
        def project(w_query, w_key, w_value):
            def part(n, j):
                cols = rows_at(j * TILE, TILE)
                source = (w_query_hbm, w_key_hbm, w_value_hbm)[n]
                return pltpu.make_async_copy(
                    source.at[:, cols], (w_query, w_key, w_value)[n].at[:, cols], part_sems.at[n, j])

            for j in range(blocks):
                for n in range(3):
                    part(n, j).start()
            for copy in own:
                copy.start()
            load_output.start()
            bias[mp] = jnp.broadcast_to(b_in[...].astype(F32)[None, :], (8, hidden))
            mask_block(length[0], mask_ref, mask_cols)
            load(tokens_hbm, rows_in, 0).wait()

            def columns(j):
                cols = rows_at(j * TILE, TILE)
                part(0, j).wait()
                out = jnp.dot(rows_in[...], w_query[:, cols], preferred_element_type=F32)
                query_t[cols, :] = (out * (LOG2E / math.sqrt(HEAD))).astype(BF).T
                part(1, j).wait()
                out = jnp.dot(rows_in[...], w_key[:, cols], preferred_element_type=F32).astype(BF)
                key[:, cols] = out
                key_t[cols, :] = out.T
                part(2, j).wait()
                out = jnp.dot(rows_in[...], w_value[:, cols], preferred_element_type=F32).astype(BF)
                value[:, cols] = out
                value_t[cols, :] = out.T

            columns(0)
            pl.semaphore_wait(barrier, shards - 1 + dp_size - 1)
            weights.start()
            for d in range(1, shards):
                bias_copy(d).start()
            for j in range(1, blocks):
                columns(j)

        pl.run_scoped(project, *[pltpu.VMEM((width, width), BF)] * 3)
        long = pltpu.VMEM((SLOT + PREFIX, SLOT), F32)
        kept = pltpu.VMEM((SLOT, SLOT), BF)
        pl.run_scoped(functools.partial(attend, key, value_t, mask_cols), long, long, kept, kept,
                      pltpu.VMEM((2 * HEAD, SLOT), F32), pltpu.VMEM((8, SLOT), F32))

    def attend(key, value_t, mask_cols, scores_a, scores_b, kept_a, kept_b, sums, totals):
        prefix_rows = slice(SLOT, SLOT + PREFIX)

        def right_side(h, half):
            q = query_t[rows_at(h * HEAD, HEAD), :]
            zero = jnp.zeros_like(q)
            last = jnp.concatenate([ones_rows(SLOT), jnp.zeros((112, SLOT), BF)], axis=0)
            return jnp.concatenate([q, zero, last] if half == 0 else [zero, q, last], axis=0)

        def folded(s):
            return jnp.max(s.reshape(s.shape[0] // 8, 8, SLOT), axis=0)

        def score_tile(h, t, right, scores, peak):
            rows = block(t)
            pair = rows_at((h // 2) * 128, 128)
            left = jnp.concatenate([key[rows, pair], mask_cols[rows, :]], axis=1)
            s = jnp.dot(left, right, preferred_element_type=F32)
            scores[rows, :] = s
            peak = folded(s) if peak is None else jnp.maximum(peak, folded(s))
            if t == blocks - 1:
                left = jnp.concatenate([prefix_key[:, pair], jnp.zeros((PREFIX, 128), BF)], axis=1)
                s = jnp.dot(left, right, preferred_element_type=F32)
                scores[prefix_rows, :] = s
                peak = jnp.maximum(peak, folded(s))
            return peak

        def set_peak(half, peak):
            peaks[half : half + 1, :] = jnp.max(peak, axis=0, keepdims=True)

        def head_step(h, half, scores_new, scores_old, kept, more):
            if more:
                right = right_side(h + 1, 1 - half)
            top = peaks[half : half + 1, :]
            rows_h = rows_at(h * HEAD, HEAD)
            left = jnp.concatenate([value_t[rows_h, :], ones_rows(SLOT)], axis=0)
            total = jnp.zeros((80, SLOT), F32)
            peak = None
            for t in range(blocks):
                rows = block(t)
                if more:
                    peak = score_tile(h + 1, t, right, scores_new, peak)
                p = jnp.exp2(scores_old[rows, :] - top).astype(BF)
                kept[rows, :] = p
                total += jnp.dot(left[:, rows], p, preferred_element_type=F32)
            kept_prefix[rows_h, :] = jnp.exp2(scores_old[prefix_rows, :] - top).astype(BF)
            if more:
                set_peak(1 - half, peak)
            sums[half * HEAD : (half + 1) * HEAD, :] = total[:HEAD]
            totals[half : half + 1, :] = total[HEAD : HEAD + 1]

        def finish_pair(i):
            pair = rows_at(i * 128, 128)
            row = lax.broadcasted_iota(jnp.int32, (128, 256), 0) // HEAD
            column = lax.broadcasted_iota(jnp.int32, (128, 256), 1)
            part = prefix_value[:, pair]
            both = jnp.concatenate([part, part], axis=0)
            both = jnp.concatenate([both, jnp.ones((128, 128), BF)], axis=1)
            wanted = jnp.where(column < 128, column // HEAD, column - 128)
            left = jnp.where(row == wanted, both, jnp.zeros_like(both))
            extra = dg(left, kept_prefix[pair, :], 0, 0)
            for n in range(2):
                scale = 1.0 / (totals[n : n + 1, :] + extra[128 + n : 129 + n, :])
                inverse[pl.ds(2 * i + n, 1), :] = scale
                own_rows = slice(n * HEAD, (n + 1) * HEAD)
                context_t[rows_at((2 * i + n) * HEAD, HEAD), :] = (
                    (sums[own_rows, :] + extra[own_rows, :]) * scale
                ).astype(BF)

        def keep(h, half):
            return pltpu.make_async_copy((kept_a, kept_b)[half], kept_hbm.at[h], keep_sems.at[half])

        right = right_side(0, 0)
        peak = None
        for t in range(blocks):
            peak = score_tile(0, t, right, scores_a, peak)
        set_peak(0, peak)

        @pl.loop(0, HEADS // 2 - 1)
        def _(i):
            h = i * 2

            @pl.when(i > 0)
            def _():
                keep(h - 2, 0).wait()
            head_step(h, 0, scores_b, scores_a, kept_a, True)
            keep(h, 0).start()

            @pl.when(i > 0)
            def _():
                keep(h - 1, 1).wait()
            head_step(h + 1, 1, scores_a, scores_b, kept_b, True)
            keep(h + 1, 1).start()
            finish_pair(i)
            for n, event in HOPS_IN_LOOP:
                @pl.when(i == n)
                def _():
                    weights.hops((event,))

        h = HEADS - 2
        keep(h - 2, 0).wait()
        head_step(h, 0, scores_b, scores_a, kept_a, True)
        keep(h, 0).start()
        keep(h - 1, 1).wait()
        head_step(h + 1, 1, scores_a, scores_b, kept_b, False)
        keep(h + 1, 1).start()
        finish_pair(HEADS // 2 - 1)
        keep(h, 0).wait()
        keep(h + 1, 1).wait()

    pl.run_scoped(attention, square, square, pltpu.VMEM((SLOT, 128), BF))
    weights.hops(HOPS_AT["attended"])


    def feed_forward(unit, inverse_one, low, active_even, active_odd, slope):
        active = (active_even, active_odd)
        gain_1, shift_1, gain_2, shift_2 = [
            ref[...].astype(F32)[None, :] for ref in (gain_one, shift_one, gain_two, shift_two)]
        everything = slice(0, SLOT)

        def shard_at(j):
            return weights.shard(j // 2, (weights.core + j) % 2)

        def mix(r):
            rs = block(r)
            summed[rs, :] = rows_in[rs, :].astype(F32) + dg(context_t[:, rs], w_output[...], 0, 0)

        def norm_one(r):
            rs = block(r)
            u, inv = norm_parts(summed[rs, :])
            unit[rs, :] = u
            inverse_one[rs, :] = inv
            normed = u * gain_1 + shift_1
            summed[rs, :] = normed
            low[rs, :] = normed.astype(BF)

        def first(j, rs, cols):
            s = shard_at(j)
            pre = jnp.dot(low[rs, :], w_in[s, :, cols], preferred_element_type=F32) + bias[s, 0:1, cols]
            act, slo = gelu_parts(pre)
            active[j % 2][rs, cols] = act
            slope[j, rs, cols] = slo

        def second(j, rs, cols):
            summed[rs, cols] += jnp.dot(active[j % 2][rs, :], w_out[shard_at(j), :, cols], preferred_element_type=F32)

        def norm_two(r):
            rs = block(r)
            u, inv = norm_parts(summed[rs, :])
            upper = norm_back(rows_in[rs, :].astype(F32) * gain_2, u, inv)
            rows_in[rs, :] = (u * gain_2 + shift_2).astype(BF)
            summed[rs, :] = upper
            low[rs, :] = upper.astype(BF)

        def third(j, rs, cols):
            grad = dg(low[rs, :], w_out[shard_at(j), cols, :], 1, 1)
            active[j % 2][rs, cols] = (grad * slope[j, rs, cols].astype(F32)).astype(BF)

        def fourth(j, rs, cols):
            summed[rs, cols] += dg(active[j % 2][rs, :], w_in[shard_at(j), cols, :], 1, 1)

        def norm_one_back(r):
            rs = block(r)
            grad = norm_back(summed[rs, :] * gain_1, unit[rs, :], inverse_one[rs, :])
            summed[rs, :] = grad
            low[rs, :] = grad.astype(BF)

        def parts(function, j, size):
            return [functools.partial(function, j, everything, slice(c, c + TILE)) for c in range(0, size, TILE)]

        def hops(j):
            return [functools.partial(weights.hops, HOPS_AT.get((j, n), ())) for n in range(width // TILE)]

        load_output.wait()
        own[0].wait()
        staged_run([mix, norm_one, lambda r: first(0, block(r), slice(0, hidden))], blocks,
                   lambda step: weights.hops(HOPS_AT.get(("mix", step), ())))
        load_grads.start()
        for d in range(1, shards):
            bias_arrival(d).wait_recv()
        own[1].wait()
        for j in range(1, shards):
            weights.ready(0, j)
            weights.ready(1, j - 1)
            interleave(parts(first, j, hidden), parts(second, j - 1, width), hops(j))
        last = shards - 1
        weights.ready(1, last)
        load_grads.wait()

        whole = slice(0, width)
        staged_run([lambda r: second(last, block(r), whole), norm_two,
                    lambda r: third(0, block(r), slice(0, hidden))], blocks)
        store_output.start()
        for j in range(1, shards):
            interleave(parts(third, j, hidden), parts(fourth, j - 1, width))
        def context_back(r):
            rs = block(r)
            grad = dg(w_output[...], low[rs, :], 1, 1)
            row = lax.broadcasted_iota(jnp.int32, (16, TILE), 0)
            for h in range(HEADS):
                rows_h = slice(h * HEAD, (h + 1) * HEAD)
                scaled = grad[rows_h, :] * inverse[h : h + 1, rs]
                middle = -jnp.sum(scaled * context_t[rows_h, rs].astype(F32), axis=0, keepdims=True)
                context_t[rows_h, rs] = scaled.astype(BF)
                high = middle.astype(BF).astype(F32)
                both = jnp.where(row == 0, high, jnp.where(row == 1, middle - high, 0.0))
                centre[h * 16 : (h + 1) * 16, rs] = both.astype(BF)

        staged_run([lambda r: fourth(last, block(r), whole), norm_one_back, context_back], blocks)

    pl.run_scoped(feed_forward, tall, pltpu.VMEM((SLOT, 1), F32), square,
                  pltpu.VMEM((SLOT, hidden), BF), pltpu.VMEM((SLOT, hidden), BF),
                  pltpu.VMEM((shards, SLOT, hidden), BF))
    weights.finish()
    for d in range(1, shards):
        bias_copy(d).wait_send()


    grad_t = context_t

    def group_copy(d):
        return remote(pieces.at[group_peer(d)], from_group.at[mp], group_sems, d, (dp, group_peer(d)))

    def group_arrival(d):
        place = from_group.at[group_sender(d)]
        return remote(place, place, group_sems, d, (dp, group_peer(d)))

    def rows_copy(d):
        return remote(from_rows.at[dp], from_rows.at[dp], rows_sems, d, ((dp + d) % dp_size, mp))

    def rows_arrival(d):
        place = from_rows.at[(dp - d + dp_size) % dp_size]
        return remote(place, place, rows_sems, d, ((dp + d) % dp_size, mp))

    def attend_back(query_back, key_back, value_back, query_prefix, staged):
        store_lower.start()

        def copy_in(h, half):
            return pltpu.make_async_copy(kept_hbm.at[h], staged.at[half], keep_sems.at[half])

        def stores(i):
            rows = rows_at(i * 128, 128)
            return [pltpu.make_async_copy(source.at[rows, :], target.at[rows, :], back_sems.at[n, i])
                    for n, (source, target) in enumerate(
                        ((query_back, query_back_hbm), (key_back, key_back_hbm), (value_back, value_back_hbm)))]

        copy_in(0, 0).start()

        def prefix_back(g):
            cols = rows_at(g * 256, 256)
            grads = grad_t[cols, :]
            back = jnp.dot(block_diagonal(prefix_value[:, cols]), grads, preferred_element_type=F32)
            parts = []
            for i in range(GROUP):
                h = g * GROUP + i
                middle = jnp.sum(centre[rows_at(h * 16, 16), :].astype(F32), axis=0, keepdims=True)
                kept = kept_prefix[rows_at(h * HEAD, HEAD), :].astype(F32)
                parts.append((kept * (back[i * HEAD : (i + 1) * HEAD] + middle)).astype(BF))
            back = jnp.concatenate(parts, axis=0)
            prefix_grads[:PREFIX, cols] = diagonal_rows(dg(back, query_t[cols, :], 1, 1)) * ln2
            prefix_grads[PREFIX:, cols] = diagonal_rows(dg(kept_prefix[cols, :], grads, 1, 1))
            query_prefix[cols, :] = dg(block_diagonal(prefix_key[:, cols]), back, 0, 0)

        for g in range(HEADS // GROUP):
            prefix_back(g)

        for s in range(shards):
            pieces[s] = prefix_grads[:, s * share : (s + 1) * share]
        for d in range(1, shards):
            group_copy(d).start()

        lane = lax.broadcasted_iota(jnp.int32, (TILE, 128), 1)
        pick = jnp.where(lane < 2, 1.0, 0.0).astype(BF)

        def head_step(h, half):
            rows_h = rows_at(h * HEAD, HEAD)
            pair = rows_at((h // 2) * 128, 128)
            grads = grad_t[rows_h, :]
            zero = jnp.zeros_like(grads)
            last = jnp.concatenate([centre[rows_at(h * 16, 16), :], jnp.zeros((112, SLOT), BF)], axis=0)
            right = jnp.concatenate([grads, zero, last] if half == 0 else [zero, grads, last], axis=0)
            queries = query_t[rows_h, :]
            keys = key_t[rows_h, :]
            total = query_prefix[rows_h, :]
            for t in range(blocks):
                rows = block(t)
                left = jnp.concatenate([value[rows, pair], pick], axis=1)
                back = jnp.dot(left, right, preferred_element_type=F32)
                w = staged[half, rows, :]
                back = (back * w.astype(F32)).astype(BF)
                value_back[rows_h, rows] = dg(grads, w, 1, 1).astype(BF)
                key_back[rows_h, rows] = (dg(queries, back, 1, 1) * ln2).astype(BF)
                total += jnp.dot(keys[:, rows], back, preferred_element_type=F32)
            query_back[rows_h, :] = (total * (1.0 / math.sqrt(HEAD))).astype(BF)

        @pl.loop(0, HEADS // 2)
        def _(i):
            h = i * 2
            copy_in(h, 0).wait()
            copy_in(h + 1, 1).start()
            head_step(h, 0)
            copy_in(h + 1, 1).wait()

            @pl.when(i < HEADS // 2 - 1)
            def _():
                copy_in(h + 2, 0).start()
            head_step(h + 1, 1)
            for copy in stores(i):
                copy.start()

            @pl.when(i == 1)
            def _():
                own_piece = pieces[mp]
                for d in range(1, shards):
                    group_arrival(d).wait_recv()
                    own_piece += from_group[group_sender(d)]
                from_rows[dp] = own_piece
                for d in range(1, dp_size):
                    rows_copy(d).start()

        for d in range(1, dp_size):
            rows_arrival(d).wait_recv()
        total = from_rows[0]
        for n in range(1, dp_size):
            total += from_rows[n]
        key_share[...] = total[:PREFIX]
        value_share[...] = total[PREFIX:]
        for d in range(1, shards):
            group_copy(d).wait_send()
        for d in range(1, dp_size):
            rows_copy(d).wait_send()
        for i in range(HEADS // 2):
            for copy in stores(i):
                copy.wait()
        store_output.wait()
        store_lower.wait()

    pl.run_scoped(attend_back, square, square, square, tall, pltpu.VMEM((2, SLOT, SLOT), BF))


def finish_kernel(output_from, key_from, value_from, lower_hbm, query_back_hbm, key_back_hbm, value_back_hbm,
                  w_query_hbm, w_key_hbm, w_value_hbm, output_hbm, input_grad_hbm, key_hbm, value_hbm,
                  total, result, lower, back, weights, passing, passing_key, passing_value,
                  back_sems, weight_sems, load_sems, store_sems):
    blocks = SLOT // TILE
    sources = ((query_back_hbm, w_query_hbm), (key_back_hbm, w_key_hbm), (value_back_hbm, w_value_hbm))
    loads = [(pltpu.make_async_copy(source, back.at[n], back_sems.at[n]),
              pltpu.make_async_copy(weight, weights.at[n], weight_sems.at[n]))
             for n, (source, weight) in enumerate(sources)]
    passed = ((output_from, passing, output_hbm), (key_from, passing_key, key_hbm),
              (value_from, passing_value, value_hbm))
    fetches = [pltpu.make_async_copy(source, middle, load_sems.at[n])
               for n, (source, middle, _) in enumerate(passed)]
    stores = [pltpu.make_async_copy(middle, target, store_sems.at[blocks + n])
              for n, (_, middle, target) in enumerate(passed)]
    load_lower = pltpu.make_async_copy(lower_hbm, lower, load_sems.at[3])
    for pair in loads:
        for copy in pair:
            copy.start()
    for copy in fetches:
        copy.start()
    load_lower.start()
    for n in range(3):
        for copy in loads[n]:
            copy.wait()
        if n == 2:
            for fetch, store in zip(fetches, stores):
                fetch.wait()
                store.start()
            load_lower.wait()
        for r in range(blocks):
            rs = slice(r * TILE, (r + 1) * TILE)
            grad = dg(back[n, :, rs], weights[n], 0, 1)
            if n == 0:
                total[rs, :] = grad
            elif n == 1:
                total[rs, :] += grad
            else:
                result[rs, :] = (lower[rs, :] + total[rs, :] + grad).astype(BF)
                store = pltpu.make_async_copy(result.at[rs, :], input_grad_hbm.at[rs, :], store_sems.at[r])
                store.start()
                stores.append(store)
    for copy in stores:
        copy.wait()


def local(dp_size, shards, tokens, lengths, key_mask, w_query, w_key, w_value, w_output, norm1_gain, norm1_shift,
          w_in, b_in, w_out, norm2_gain, norm2_shift, prefix_key, prefix_value, out_grad):
    rows, width = tokens.shape
    hidden = w_in.shape[1]
    share = width // shards
    chips = shards // 2
    shape = jax.ShapeDtypeStruct
    square = pltpu.VMEM((SLOT, width), BF)
    dma = pltpu.SemaphoreType.DMA
    output, lower, query_back, key_back, value_back, key_grad, value_grad, _ = pl.pallas_call(
        functools.partial(layer_kernel, dp_size, shards),
        out_shape=[shape((rows, width), BF), shape((rows, width), F32)] + [shape((width, SLOT), BF)] * 3
        + [shape((PREFIX, share), F32)] * 2 + [shape((HEADS, SLOT, SLOT), BF)],
        in_specs=[SMEM] + [VMEM] * 8 + [HBM] * 8,
        out_specs=[HBM] * 5 + [VMEM, VMEM, HBM],
        scratch_shapes=[
            pltpu.VMEM((shards, width, hidden), BF),
            pltpu.VMEM((shards, hidden, width), BF),
            pltpu.VMEM((shards, 8, hidden), F32),
            pltpu.VMEM((shards, 2 * PREFIX, share), F32),
            pltpu.VMEM((shards, 2 * PREFIX, share), F32),
            pltpu.VMEM((dp_size, 2 * PREFIX, share), F32),
            pltpu.VMEM((SLOT, width), F32),
            square, square, square, square, square, square, square,
            pltpu.VMEM((HEADS, SLOT), F32),
            pltpu.VMEM((HEADS * 16, SLOT), BF),
            pltpu.VMEM((8, SLOT), F32),
            pltpu.VMEM((2 * PREFIX, width), F32),
            dma((2, 8, 4 if chips <= 2 else 2, max(chips, 2))),
            dma((2, 2)),
            dma((2, shards)),
            dma((2, shards)),
            dma((2, dp_size)),
            dma((3, SLOT // TILE)),
            dma((8,)),
            dma((2,)),
            dma((2,)),
            dma((3, HEADS // 2)),
        ],
        compiler_params=pltpu.CompilerParams(
            vmem_limit_bytes=63 * 2**20, collective_id=0, has_side_effects=True),
        cost_estimate=pl.CostEstimate(flops=70 * 10**9, bytes_accessed=10**8, transcendentals=3 * 10**7),
        name="layer",
    )(lengths, key_mask.reshape(1, SLOT), norm1_gain, norm1_shift, norm2_gain, norm2_shift, b_in, prefix_key, prefix_value,
      tokens, w_query, w_key, w_value, w_output, w_in, w_out, out_grad)
    return pl.pallas_call(
        finish_kernel,
        out_shape=[shape((rows, width), BF)] * 2 + [shape((PREFIX, share), F32)] * 2,
        in_specs=[HBM] * 10,
        out_specs=[HBM] * 4,
        scratch_shapes=[
            pltpu.VMEM((SLOT, width), F32),
            square,
            pltpu.VMEM((SLOT, width), F32),
            pltpu.VMEM((3, width, SLOT), BF),
            pltpu.VMEM((3, width, width), BF),
            square,
            pltpu.VMEM((PREFIX, share), F32),
            pltpu.VMEM((PREFIX, share), F32),
            dma((3,)),
            dma((3,)),
            dma((4,)),
            dma((SLOT // TILE + 3,)),
        ],
        compiler_params=pltpu.CompilerParams(vmem_limit_bytes=60 * 2**20),
        cost_estimate=pl.CostEstimate(flops=7 * 10**9, bytes_accessed=3 * 10**7, transcendentals=0),
        name="finish",
    )(output, key_grad, value_grad, lower, query_back, key_back, value_back, w_query, w_key, w_value)


def solution(mesh):
    in_specs = (
        P(("dp", "mp"), None), P(("dp", "mp")), P(("dp", "mp")), P(), P(), P(), P(), P(), P(),
        P(None, "mp"), P("mp"), P("mp", None), P(), P(), P(), P(), P(("dp", "mp"), None),
    )
    out_specs = (P(("dp", "mp"), None), P(("dp", "mp"), None), P(None, "mp"), P(None, "mp"))
    return jax.shard_map(
        functools.partial(local, mesh.shape["dp"], mesh.shape["mp"]),
        mesh=mesh, in_specs=in_specs, out_specs=out_specs, check_vma=False)
```
